32 devices in a mesh: dp: 2 (over y), expert: 16 (over z, x, core).
Axes of the slice: x: 2, y: 2, z: 4, core: 2. Of those that a mesh axis runs over, the one named last changes fastest.
Arguments:
- tokens: bfloat16 [2048, 1024], P('expert'), may hold values from -6 to 6
- routes: int32 [2048, 6], P('expert'), may hold values from 0 to 15, all different within a row; in each aligned block of 128 rows (0 to 127, 128 to 255, ...) at most 64 rows name the same one
- route_gates: bfloat16 [2048, 6], P('expert'), may hold values from 0.049804688 to 0.5
- domains: int32 [2048], P('expert'), may hold values from 0 to 63
- domain_weight: float32 [64], replicated, may hold values from 0.25 to 4
- targets: bfloat16 [2048, 1024], P('expert'), may hold values from -6 to 6
- w_gate: bfloat16 [16, 1024, 1024], P('expert', None, 'dp'), may hold values from -0.1875 to 0.1875
- w_up: bfloat16 [16, 1024, 1024], P('expert', None, 'dp'), may hold values from -0.1875 to 0.1875
- w_down: bfloat16 [16, 1024, 1024], P('expert', 'dp'), may hold values from -0.1875 to 0.1875
Outputs:
- grad_tokens: bfloat16 [2048, 1024], P('expert')
- grad_gate: float32 [16, 1024, 1024], P('expert', None, 'dp')
- grad_up: float32 [16, 1024, 1024], P('expert', None, 'dp')
- grad_down: float32 [16, 1024, 1024], P('expert', 'dp')
The draws below stay inside these ranges and needn't reach their ends.
Inputs may be any that keep to these rules, and one draw needn't show every extreme that they name: `routes`: each row names 6 different experts. Among the rows of one block of 128 tokens no expert is named more than 64 times, and in every draw some block names some expert exactly 64 times.
All inputs are finite; a program needn't handle non-finite values.
Results may differ from the reference program's by a relative error of at most 0.015.
Values may be sent and summed in bfloat16 or wider, within the bound.
A program may use at most 64 MiB of HBM per device.

```python
import math
import jax
import jax.numpy as jnp
import numpy as np
from jax import lax

D = 1024
FF = 1024
TOPK = 6
NDOM = 64
TOK_DEV = 128
EXPERTS = 16
CAP = 64
FF_DEV = 512
SLOTS = 1024
TOKENS = 2048
N_DP = 2


def with_ends(array, own_key, low, largest):
    longest = array.shape.index(max(array.shape))
    spots = []
    for shift in (0, 1):
        where = [jax.random.randint(jax.random.fold_in(own_key, axis), (), 0, length) for axis, length in enumerate(array.shape)]
        where[longest] = (where[longest] + shift) % array.shape[longest]
        spots.append(tuple(where))
    return array.at[spots[0]].set(low).at[spots[1]].set(largest)


def block_levels(key, shape, cuts, smallest, high):
    def one(position, shards_of):
        draws = jax.random.uniform(jax.random.fold_in(jax.random.fold_in(key, 6), position), (shards_of,), jnp.float32, smallest / len(cuts), high / len(cuts))
        return jnp.repeat(jnp.exp(draws), shape[position] // shards_of).reshape((-1,) + (1,) * (len(shape) - position - 1))

    loudness = one(*cuts[0])
    for cut in cuts[1:]:
        loudness = loudness * one(*cut)
    return loudness


def assign_block(key, own, number, rows, count, top, bound, lean):
    order = jax.random.permutation(key, count)
    crowded, ordinary = load_shares(count, rows * top, bound, lean, True), load_shares(count, rows * top, bound, lean, False)
    places = jnp.arange(count)

    def named(tallies, rotation):
        used = int((tallies > 0).sum())
        fixed = max(1, used // 4)
        moved = fixed + (places - fixed + rotation * (used - fixed)) % max(1, count - fixed)
        return jnp.zeros((count,), jnp.int32).at[order[jnp.where(places < fixed, places, moved)]].set(jnp.asarray(tallies, jnp.int32))

    tallies = jnp.where(number % 4 == 0, named(crowded, number // 4), named(ordinary, number - number // 4 - 1))
    mixed = jax.random.permutation(jax.random.fold_in(own, 3), count)
    giver, sink = mixed[0:count // 2 * 2:2], mixed[1:count // 2 * 2:2]
    room = jnp.minimum(tallies[giver] - 1, bound - tallies[sink]) // 2
    room = jnp.where((giver == order[0]) | (sink == order[0]) | (tallies[sink] == 0), 0, jnp.maximum(room, 0))
    moved = jax.random.randint(jax.random.fold_in(own, 4), (count // 2,), 0, 1 << 20) % (room + 1)
    tallies = tallies.at[giver].add(-moved).at[sink].add(moved)
    items = jnp.searchsorted(jnp.cumsum(tallies), jnp.arange(rows * top), side="right").astype(jnp.int32)
    listing = items.reshape(top, rows).T
    listing = listing[jax.random.permutation(jax.random.fold_in(own, 1), rows)]
    rotation = jax.random.randint(jax.random.fold_in(own, 2), (rows, 1), 0, top)
    return jnp.take_along_axis(listing, (jnp.arange(top)[None, :] + rotation) % top, axis=1)


def load_shares(number_of, total, reach, lean, full):
    loads = [(1 << 20) // math.isqrt(grade ** lean) + 1 for grade in range(1, number_of + 1)]
    largest = reach if full else min(reach, max(-(-total // number_of), total * loads[0] // sum(loads)))
    least = 1 if total - largest >= number_of - 1 else 0
    counts, surplus = [largest] + [least] * (number_of - 1), total - largest - least * (number_of - 1)
    while surplus > 0:
        candidates = [i for i in range(1, number_of) if counts[i] < largest] or [i for i in range(1, number_of) if counts[i] < reach]
        pool, remaining = sum([loads[i] for i in candidates]), surplus
        for i in candidates:
            addition = min(reach - counts[i], max(1, remaining * loads[i] // pool), surplus)
            counts[i] = counts[i] + addition
            surplus = surplus - addition
    return np.array(counts)


def scatter_about(stream_key, extent, width, most, cuts=(), kind=jnp.bfloat16):
    array = jax.random.normal(stream_key, extent, jnp.float32) * width
    if len(cuts) > 0:
        array = block_levels(stream_key, extent, cuts, -0.22, 0.18) * array
    return jnp.clip(array, min=-most, max=most).astype(kind)


def setup_inputs(seed: int = 0) -> dict:
    key_list = jax.random.split(jax.random.key(seed), 10)
    tokens = scatter_about(key_list[0], (TOKENS, D), 1.0, 6.0, ((0, 16),))
    routes_keys = jax.random.split(jax.random.fold_in(key_list[1], 1), TOKENS // TOK_DEV)
    routes_turns = jax.random.permutation(jax.random.fold_in(key_list[1], 3), TOKENS // TOK_DEV)
    routes = jax.vmap(lambda own, number: assign_block(jax.random.fold_in(key_list[1], 2), own, number, TOK_DEV, EXPERTS, TOPK, CAP, 2))(routes_keys, routes_turns).reshape((TOKENS, TOPK))
    route_gates = jnp.clip(0.049804688 + 0.4501953 * jax.random.uniform(key_list[2], (TOKENS, TOPK), jnp.float32) ** block_levels(key_list[2], (TOKENS, TOPK), ((0, 16),), -0.2, 0.2), 0.049804688, 0.5).astype(jnp.bfloat16)
    domains = with_ends(jax.random.randint(key_list[3], (TOKENS,), 0, NDOM), jax.random.fold_in(key_list[3], 1), 0, NDOM - 1).astype(jnp.int32)
    domain_weight = jnp.clip(jnp.exp(jax.random.uniform(key_list[4], (NDOM,), jnp.float32, math.log(0.25), math.log(4.0))), 0.25, 4.0)
    targets = scatter_about(key_list[5], (TOKENS, D), 1.0, 6.0, ((0, 16),))
    w_gate = scatter_about(key_list[6], (EXPERTS, D, FF), D ** -0.5, 0.1875, ((0, 16), (2, 2)))
    w_up = scatter_about(key_list[7], (EXPERTS, D, FF), D ** -0.5, 0.1875, ((0, 16), (2, 2)))
    w_down = scatter_about(key_list[8], (EXPERTS, FF, D), FF ** -0.5, 0.1875, ((0, 16), (1, 2)))
    return {"tokens": tokens, "routes": routes, "route_gates": route_gates, "domains": domains, "domain_weight": domain_weight, "targets": targets, "w_gate": w_gate, "w_up": w_up, "w_down": w_down}


def slot_layout(routes, route_gates):
    blocks = TOKENS // TOK_DEV
    per_block = TOK_DEV * TOPK
    flat_routes = routes.reshape(blocks, per_block).astype(jnp.int32)
    onehot = (flat_routes[:, :, None] == jnp.arange(EXPERTS, dtype=jnp.int32)[None, None, :]).astype(jnp.int32)
    places = jnp.sum((jnp.cumsum(onehot, 1) - onehot) * onehot, 2).astype(jnp.int32)
    block_ids = jnp.arange(blocks, dtype=jnp.int32)[:, None]
    slot_ids = (flat_routes * SLOTS + block_ids * CAP + places).astype(jnp.int32).reshape(-1)
    token_ids = (block_ids * TOK_DEV + (jnp.arange(per_block, dtype=jnp.int32) // TOPK)[None, :]).astype(jnp.int32).reshape(-1)
    slot_token = jnp.full((EXPERTS * SLOTS,), TOKENS, jnp.int32).at[slot_ids].set(token_ids)
    slot_gate = jnp.zeros((EXPERTS * SLOTS,), jnp.float32).at[slot_ids].set(route_gates.reshape(-1).astype(jnp.float32))
    return slot_token, slot_gate


def block_sum(pieces):
    return jnp.sum(lax.optimization_barrier(pieces.astype(jnp.bfloat16)).astype(jnp.float32), 0)


def expert_forward(slot_rows, gate_w, up_w, down_w):
    gate_pre = jnp.dot(slot_rows, gate_w, preferred_element_type=jnp.float32)
    up_pre = jnp.dot(slot_rows, up_w, preferred_element_type=jnp.float32)
    hidden = (jax.nn.silu(gate_pre) * up_pre).astype(jnp.bfloat16)
    pieces = jnp.einsum("rsf,sfd->srd", hidden.astype(jnp.float32).reshape(SLOTS, N_DP, FF_DEV),
                        down_w.astype(jnp.float32).reshape(N_DP, FF_DEV, D), precision=lax.Precision.HIGHEST)
    return gate_pre, up_pre, hidden, block_sum(pieces)


def expert_backward(slot_rows, slot_grads, gate_w, up_w, down_w):
    gate_pre, up_pre, hidden, unused = expert_forward(slot_rows, gate_w, up_w, down_w)
    hidden_grad = jnp.dot(slot_grads, down_w.T, preferred_element_type=jnp.float32)
    sigma = jax.nn.sigmoid(gate_pre)
    gate_grad = (hidden_grad * up_pre * sigma * (1.0 + gate_pre * (1.0 - sigma))).astype(jnp.bfloat16)
    up_grad = (hidden_grad * gate_pre * sigma).astype(jnp.bfloat16)
    grad_down = jnp.dot(hidden.T, slot_grads, preferred_element_type=jnp.float32)
    grad_gate = jnp.dot(slot_rows.T, gate_grad, preferred_element_type=jnp.float32)
    grad_up = jnp.dot(slot_rows.T, up_grad, preferred_element_type=jnp.float32)
    gate_part = jnp.einsum("rsf,dsf->srd", gate_grad.astype(jnp.float32).reshape(SLOTS, N_DP, FF_DEV),
                           gate_w.astype(jnp.float32).reshape(D, N_DP, FF_DEV), precision=lax.Precision.HIGHEST)
    up_part = jnp.einsum("rsf,dsf->srd", up_grad.astype(jnp.float32).reshape(SLOTS, N_DP, FF_DEV),
                         up_w.astype(jnp.float32).reshape(D, N_DP, FF_DEV), precision=lax.Precision.HIGHEST)
    return grad_gate, grad_up, grad_down, block_sum(gate_part + up_part)


def reference(tokens, routes, route_gates, domains, domain_weight, targets, w_gate, w_up, w_down):
    slot_token, slot_gate = slot_layout(routes, route_gates)
    padded = jnp.concatenate([tokens, jnp.zeros((1, D), jnp.bfloat16)], 0)
    slot_rows = padded[slot_token].reshape(EXPERTS, SLOTS, D)

    def forward_one(items):
        return expert_forward(items[0], items[1], items[2], items[3])[3]

    slot_out = lax.map(forward_one, (slot_rows, w_gate, w_up, w_down))
    weighted = slot_gate[:, None] * slot_out.reshape(EXPERTS * SLOTS, D)
    layer_out = jax.ops.segment_sum(weighted, slot_token, TOKENS + 1)[:TOKENS]
    scales = domain_weight[domains]
    loss_grad = (scales[:, None] * (layer_out - targets.astype(jnp.float32))).astype(jnp.bfloat16)
    grad_padded = jnp.concatenate([loss_grad.astype(jnp.float32), jnp.zeros((1, D), jnp.float32)], 0)
    slot_grads = (slot_gate[:, None] * grad_padded[slot_token]).astype(jnp.bfloat16).reshape(EXPERTS, SLOTS, D)

    def backward_one(items):
        return expert_backward(items[0], items[1], items[2], items[3], items[4])

    grad_gate, grad_up, grad_down, row_sums = lax.map(backward_one, (slot_rows, slot_grads, w_gate, w_up, w_down))
    grad_tokens = jax.ops.segment_sum(row_sums.reshape(EXPERTS * SLOTS, D), slot_token, TOKENS + 1)[:TOKENS]
    return grad_tokens.astype(jnp.bfloat16), grad_gate, grad_up, grad_down
```

```python
import functools

import jax
import jax.numpy as jnp
from jax import lax
from jax.experimental import pallas as pl
from jax.experimental.pallas import tpu as pltpu
from jax.sharding import PartitionSpec as P

MESH = pl.DeviceIdType.MESH
CORES = 2
COLUMNS = 2
HALVES = 2
UP, DOWN, ACROSS, SIBLING = range(4)


class Place:
    def __init__(self, n):
        self.n = n
        self.height = n // (CORES * COLUMNS)
        self.me = lax.axis_index("expert")
        self.core = lax.rem(self.me, CORES)
        self.x = lax.rem(self.me // CORES, COLUMNS)
        self.z = self.me // (CORES * COLUMNS)
        self.up = self.me + CORES * COLUMNS
        self.down = self.me - CORES * COLUMNS
        self.has_up = self.z + 1 < self.height
        self.has_down = self.z > 0
        self.across = self.at(self.z, 1 - self.x, self.core)
        self.sibling = self.at(self.z, self.x, 1 - self.core)

    def at(self, z, x, core):
        return (z * COLUMNS + x) * CORES + core

    def by_distance(self, d):
        if d == 0:
            return [(self.z, None)]
        return [(self.z - d, self.z - d >= 0), (self.z + d, self.z + d < self.height)]


def when(condition, body):
    if condition is None:
        body()
    else:
        pl.when(condition)(body)


def greet(place, dp_too):
    barrier = pltpu.get_barrier_semaphore()

    def signal(target):
        pl.semaphore_signal(barrier, inc=1, device_id=target, device_id_type=MESH)

    pl.when(place.has_up)(lambda: signal({"expert": place.up}))
    pl.when(place.has_down)(lambda: signal({"expert": place.down}))
    signal({"expert": place.across})
    signal({"expert": place.sibling})
    count = 2 + place.has_up.astype(jnp.int32) + place.has_down.astype(jnp.int32)
    if dp_too:
        dps = lax.axis_size("dp")
        mine = lax.axis_index("dp")
        for step in range(1, dps):
            signal({"dp": lax.rem(mine + step, dps)})
        count = count + (dps - 1)
    pl.semaphore_wait(barrier, count)


def gather(place, pieces, send, recv):
    links = {
        UP: (place.up, place.has_up),
        DOWN: (place.down, place.has_down),
        ACROSS: (place.across, None),
        SIBLING: (place.sibling, None),
    }

    def copy(piece, block, link):
        view = pieces[piece](block)
        return pltpu.make_async_remote_copy(
            src_ref=view,
            dst_ref=view,
            send_sem=send.at[piece, link, block],
            recv_sem=recv.at[piece, block],
            device_id={"expert": links[link][0]},
            device_id_type=MESH,
        )

    def start(piece, block, which):
        for link in which:
            when(links[link][1], lambda link=link: copy(piece, block, link).start())

    def arrive(piece, block):
        copy(piece, block, SIBLING).wait_recv()

    def mine(z):
        return place.at(z, place.x, place.core)

    def other(z):
        return place.at(z, 1 - place.x, place.core)

    def from_across(d):
        for piece in range(len(pieces)):
            for z, there in place.by_distance(d):

                def body(z=z, piece=piece):
                    arrive(piece, other(z))
                    start(piece, other(z), (SIBLING,))

                when(there, body)

    for piece in range(len(pieces)):
        start(piece, place.me, (UP, DOWN, ACROSS, SIBLING))
    for d in range(1, place.height):
        for piece in range(len(pieces)):
            for (z, there), onward in zip(place.by_distance(d), (UP, DOWN)):

                def body(z=z, piece=piece, onward=onward):
                    arrive(piece, mine(z))
                    start(piece, mine(z), (onward, ACROSS, SIBLING))

                when(there, body)
        from_across(d - 1)
    from_across(place.height - 1)

    def finish():
        for z in range(place.height):
            for piece in range(len(pieces)):
                for x in range(COLUMNS):
                    arrive(piece, place.at(z, x, 1 - place.core))
                copy(piece, mine(z), ACROSS).wait_send()
                copy(piece, mine(z), SIBLING).wait_send()
                copy(piece, other(z), SIBLING).wait_send()
                pl.when(jnp.logical_and(place.has_up, z <= place.z))(
                    lambda: copy(piece, mine(z), UP).wait_send()
                )
                pl.when(jnp.logical_and(place.has_down, z >= place.z))(
                    lambda: copy(piece, mine(z), DOWN).wait_send()
                )

    finish()


def scatter(place, part_ref, bufs, sems, leave):
    core_in, across_out, across_in, line_out, line_in, dp_in = bufs
    core_send, core_recv, across_send, across_recv, line_send, line_recv, dp_send, dp_recv = sems
    height = place.height
    rows = part_ref.shape[1] // HALVES
    dps = lax.axis_size("dp")
    dp = lax.axis_index("dp")
    spans = [pl.ds(h * rows, rows) for h in range(HALVES)]
    f32 = jnp.float32

    def core_copy(z, x, h):
        spot = z * COLUMNS + x
        return pltpu.make_async_remote_copy(
            src_ref=part_ref.at[place.at(z, x, 1 - place.core), spans[h]],
            dst_ref=core_in.at[spot, spans[h]],
            send_sem=core_send.at[spot, h],
            recv_sem=core_recv.at[spot, h],
            device_id={"expert": place.sibling},
            device_id_type=MESH,
        )

    def across_copy(z, h):
        return pltpu.make_async_remote_copy(
            src_ref=across_out.at[z, spans[h]],
            dst_ref=across_in.at[z, spans[h]],
            send_sem=across_send.at[z, h],
            recv_sem=across_recv.at[z, h],
            device_id={"expert": place.across},
            device_id_type=MESH,
        )

    def line_copy(z, slot, h, target):
        return pltpu.make_async_remote_copy(
            src_ref=line_out.at[z, spans[h]],
            dst_ref=line_in.at[slot, spans[h]],
            send_sem=line_send.at[z, h],
            recv_sem=line_recv.at[slot, h],
            device_id={"expert": target},
            device_id_type=MESH,
        )

    def line_arrive(slot, h):
        line_copy(0, slot, h, place.up).wait_recv()

    def dp_copy(step, h):
        return pltpu.make_async_remote_copy(
            src_ref=dp_in.at[dp, spans[h]],
            dst_ref=dp_in.at[dp, spans[h]],
            send_sem=dp_send.at[step, h],
            recv_sem=dp_recv.at[dp, h],
            device_id={"dp": lax.rem(dp + step, dps)},
            device_id_type=MESH,
        )

    def dp_arrive(index, h):
        pltpu.make_async_remote_copy(
            src_ref=dp_in.at[dp, spans[h]],
            dst_ref=dp_in.at[index, spans[h]],
            send_sem=dp_send.at[1, h],
            recv_sem=dp_recv.at[index, h],
            device_id={"dp": lax.rem(dp + 1, dps)},
            device_id_type=MESH,
        ).wait_recv()

    def in_order(body):
        for d in range(height - 1, -1, -1):
            for way, (z, there) in enumerate(place.by_distance(d)):
                for h in range(HALVES):
                    when(there, lambda z=z, h=h: body(z, h, None if d == 0 else (DOWN, UP)[way]))

    def send_core(z, h, way):
        core_copy(z, 1 - place.x, h).start()

    def send_core_own(z, h, way):
        core_copy(z, place.x, h).start()

    def send_across(z, h, way):
        core_copy(z, 1 - place.x, h).wait_recv()
        span = spans[h]
        total = part_ref[place.at(z, 1 - place.x, place.core), span].astype(f32)
        total = total + core_in[z * COLUMNS + 1 - place.x, span].astype(f32)
        across_out[z, span] = total.astype(jnp.bfloat16)
        across_copy(z, h).start()

    def send_line(z, h, way):
        span = spans[h]
        core_copy(z, place.x, h).wait_recv()
        across_copy(z, h).wait_recv()

        def total():
            own = part_ref[place.at(z, place.x, place.core), span].astype(f32)
            own = own + core_in[z * COLUMNS + place.x, span].astype(f32)
            return own + across_in[z, span].astype(f32)

        if way is None:

            def store(value):
                dp_in[dp, span] = value.astype(jnp.bfloat16)

            def both():
                line_arrive(z, h)
                line_arrive(height, h)
                store(total() + line_in[z, span].astype(f32) + line_in[height, span].astype(f32))

            def above():
                line_arrive(z, h)
                store(total() + line_in[z, span].astype(f32))

            def below():
                line_arrive(height, h)
                store(total() + line_in[height, span].astype(f32))

            pl.when(jnp.logical_and(place.has_up, place.has_down))(both)
            pl.when(jnp.logical_and(place.has_up, jnp.logical_not(place.has_down)))(above)
            pl.when(jnp.logical_and(jnp.logical_not(place.has_up), place.has_down))(below)
            for step in range(1, dps):
                dp_copy(step, h).start()
            return
        if way == DOWN:
            before, slot, target = place.has_up, z, place.down
        else:
            before, target = place.has_down, place.up
            slot = jnp.where(z == place.z + 1, height, z)

        def with_arrival():
            line_arrive(z, h)
            line_out[z, span] = (total() + line_in[z, span].astype(f32)).astype(jnp.bfloat16)

        def alone():
            line_out[z, span] = total().astype(jnp.bfloat16)

        pl.when(before)(with_arrival)
        pl.when(jnp.logical_not(before))(alone)
        line_copy(z, slot, h, target).start()

    in_order(send_core)
    in_order(send_core_own)
    in_order(send_across)
    in_order(send_line)
    for h in range(HALVES):
        for step in range(1, dps):
            dp_arrive(lax.rem(dp + step, dps), h)
        total = dp_in[0, spans[h]].astype(f32)
        for index in range(1, dps):
            total = total + dp_in[index, spans[h]].astype(f32)
        leave(h, spans[h], total)

    def settle(z, h, way):
        core_copy(z, 0, h).wait_send()
        core_copy(z, 1, h).wait_send()
        across_copy(z, h).wait_send()
        if way is not None:
            line_copy(z, 0, h, place.up).wait_send()

    in_order(settle)
    for h in range(HALVES):
        for step in range(1, dps):
            dp_copy(step, h).wait_send()


def scatter_scratch(n, rows, width):
    height = n // (CORES * COLUMNS)
    dps = lax.axis_size("dp")
    sizes = [height * COLUMNS, height, height, height, height + 1, dps]
    sems = [height * COLUMNS] * 2 + [height] * 3 + [height + 1] + [dps] * 2
    return (
        [pltpu.VMEM((size, rows, width), jnp.bfloat16) for size in sizes],
        [pltpu.SemaphoreType.DMA((size, HALVES)) for size in sems],
    )


def gather_scratch(n, pieces):
    return [pltpu.SemaphoreType.DMA((pieces, 4, n)), pltpu.SemaphoreType.DMA((pieces, n))]


def token_pieces(ref):
    rows = ref.shape[1] // HALVES
    return [lambda block, h=h: ref.at[block, pl.ds(h * rows, rows)] for h in range(HALVES)]


def spread_kernel(n, tokens_ref, table_ref, rows_ref, tables_ref, send, recv):
    place = Place(n)
    rows_ref[place.me] = tokens_ref[...]
    tables_ref[place.me] = table_ref[...]
    greet(place, False)
    gather(place, [lambda block: tables_ref.at[block]] + token_pieces(rows_ref), send, recv)


def loss_kernel(n, part_ref, targets_ref, scales_ref, grads_ref, *scratch):
    place = Place(n)
    bufs, sems, (send, recv) = scratch[:6], scratch[6:14], scratch[14:]
    greet(place, True)

    def leave(h, span, total):
        error = total - targets_ref[span, :].astype(jnp.float32)
        grads_ref[place.me, span] = (scales_ref[span, :] * error).astype(jnp.bfloat16)

    scatter(place, part_ref, bufs, sems, leave)
    gather(place, token_pieces(grads_ref), send, recv)


def return_kernel(n, part_ref, out_ref, *scratch):
    place = Place(n)
    bufs, sems = scratch[:6], scratch[6:14]
    greet(place, True)

    def leave(h, span, total):
        out_ref[span, :] = total.astype(jnp.bfloat16)

    scatter(place, part_ref, bufs, sems, leave)


def run(kernel, out_shape, scratch, number, *operands):
    single = not isinstance(out_shape, (list, tuple))
    whole = pl.BlockSpec(memory_space=pltpu.VMEM)
    return pl.pallas_call(
        kernel,
        out_shape=out_shape,
        in_specs=[whole] * len(operands),
        out_specs=whole if single else [whole] * len(out_shape),
        scratch_shapes=scratch,
        compiler_params=pltpu.CompilerParams(
            collective_id=number, has_side_effects=True, vmem_limit_bytes=60 * 2**20
        ),
    )(*operands)


def table_of(routes, route_gates, experts):
    count = routes.shape[0]
    hits = routes[None, :, :] == jnp.arange(experts, dtype=jnp.int32)[:, None, None]
    chosen = jnp.any(hits, 2)
    earlier = jnp.arange(count)[:, None] < jnp.arange(count)[None, :]
    places = jnp.dot(
        chosen.astype(jnp.bfloat16), earlier.astype(jnp.bfloat16), preferred_element_type=jnp.float32
    )
    places = jnp.where(chosen, places, -1.0)
    gates = jnp.sum(jnp.where(hits, route_gates.astype(jnp.float32)[None], 0.0), 2)
    return jnp.concatenate([places, gates], 0).astype(jnp.bfloat16)


def block_dot(left, right, contract):
    return lax.dot_general(
        left, right, ((contract[0], contract[1]), ((0,), (0,))), preferred_element_type=jnp.float32
    ).astype(jnp.bfloat16)


def shards(tokens, routes, route_gates, domains, domain_weight, targets, w_gate, w_up, w_down):
    count, width = tokens.shape
    n = lax.axis_size("expert")
    capacity = max(2, 4 * count * routes.shape[1] // (3 * n))
    bf16, f32 = jnp.bfloat16, jnp.float32
    contract_last = (((1,), (1,)), ((), ()))
    contract_first = (((0,), (0,)), ((), ()))

    table = table_of(routes, route_gates, n)
    rows, tables = run(
        functools.partial(spread_kernel, n),
        [jax.ShapeDtypeStruct((n, count, width), bf16), jax.ShapeDtypeStruct((n, 2 * n, count), bf16)],
        gather_scratch(n, HALVES + 1),
        0,
        tokens,
        table,
    )
    me = lax.axis_index("expert")
    places = lax.dynamic_index_in_dim(tables, me, 1, keepdims=True)
    gates = lax.dynamic_index_in_dim(tables, me + n, 1, keepdims=True)
    matches = places.astype(jnp.int32) == jnp.arange(capacity, dtype=jnp.int32)[None, :, None]
    select = matches.astype(bf16)
    gated = jnp.where(matches, gates, jnp.zeros((), bf16))

    slot_rows = block_dot(select, rows, ((2,), (1,))).reshape(n * capacity, width)
    gate_pre = jnp.dot(slot_rows, w_gate[0], preferred_element_type=f32)
    up_pre = jnp.dot(slot_rows, w_up[0], preferred_element_type=f32)
    hidden = (jax.nn.silu(gate_pre) * up_pre).astype(bf16)
    part = jnp.dot(hidden, w_down[0], preferred_element_type=f32).astype(bf16)
    outs = block_dot(gated, part.reshape(n, capacity, width), ((1,), (1,)))

    picks = domains[:, None] == jnp.arange(domain_weight.shape[0], dtype=jnp.int32)[None, :]
    scales = jnp.sum(jnp.where(picks, domain_weight[None, :], 0.0), 1, keepdims=True)
    bufs, sems = scatter_scratch(n, count, width)
    loss_grads = run(
        functools.partial(loss_kernel, n),
        jax.ShapeDtypeStruct((n, count, width), bf16),
        bufs + sems + gather_scratch(n, HALVES),
        1,
        outs,
        targets,
        scales,
    )

    slot_grads = block_dot(gated, loss_grads, ((2,), (1,))).reshape(n * capacity, width)
    hidden_grad = lax.dot_general(slot_grads, w_down[0], contract_last, preferred_element_type=f32)
    sigma = jax.nn.sigmoid(gate_pre)
    gate_grad = (hidden_grad * up_pre * sigma * (1.0 + gate_pre * (1.0 - sigma))).astype(bf16)
    up_grad = (hidden_grad * gate_pre * sigma).astype(bf16)
    row_part = lax.dot_general(gate_grad, w_gate[0], contract_last, preferred_element_type=f32)
    row_part = row_part + lax.dot_general(up_grad, w_up[0], contract_last, preferred_element_type=f32)
    backs = block_dot(select, row_part.astype(bf16).reshape(n, capacity, width), ((1,), (1,)))
    grad_tokens = run(
        functools.partial(return_kernel, n),
        jax.ShapeDtypeStruct((count, width), bf16),
        bufs + sems,
        2,
        backs,
    )
    grad_down = lax.dot_general(hidden, slot_grads, contract_first, preferred_element_type=f32)
    grad_gate = lax.dot_general(slot_rows, gate_grad, contract_first, preferred_element_type=f32)
    grad_up = lax.dot_general(slot_rows, up_grad, contract_first, preferred_element_type=f32)
    return grad_tokens, grad_gate[None], grad_up[None], grad_down[None]


def solution(mesh):
    return jax.shard_map(
        shards,
        mesh=mesh,
        in_specs=(
            P("expert", None),
            P("expert", None),
            P("expert", None),
            P("expert"),
            P(),
            P("expert", None),
            P("expert", None, "dp"),
            P("expert", None, "dp"),
            P("expert", "dp", None),
        ),
        out_specs=(
            P("expert", None),
            P("expert", None, "dp"),
            P("expert", None, "dp"),
            P("expert", "dp", None),
        ),
        check_vma=False,
    )
```

```python
import functools

import jax
import jax.numpy as jnp
from jax import lax
from jax.experimental import pallas as pl
from jax.experimental.pallas import tpu as pltpu
from jax.sharding import PartitionSpec as P

MESH = pl.DeviceIdType.MESH
CORES = 2
COLUMNS = 2
PIECES = 4
UP, DOWN, ACROSS, SIBLING, PARTNER = range(5)


class Place:
    def __init__(self, n):
        self.n = n
        self.height = n // (CORES * COLUMNS)
        self.me = lax.axis_index("expert")
        self.core = lax.rem(self.me, CORES)
        self.x = lax.rem(self.me // CORES, COLUMNS)
        self.z = self.me // (CORES * COLUMNS)
        self.up = self.me + CORES * COLUMNS
        self.down = self.me - CORES * COLUMNS
        self.has_up = self.z + 1 < self.height
        self.has_down = self.z > 0
        self.parity = lax.rem(lax.axis_index("dp"), 2)
        self.partner = lax.axis_index("dp") + 1 - 2 * self.parity
        self.across = self.at(self.z, 1 - self.x, self.core)
        self.sibling = self.at(self.z, self.x, 1 - self.core)

    def at(self, z, x, core):
        return (z * COLUMNS + x) * CORES + core

    def by_distance(self, d):
        if d == 0:
            return [(self.z, None)]
        return [(self.z - d, self.z - d >= 0), (self.z + d, self.z + d < self.height)]


def when(condition, body):
    if condition is None:
        body()
    else:
        pl.when(condition)(body)


def greet(place):
    barrier = pltpu.get_barrier_semaphore()

    def signal(target):
        pl.semaphore_signal(barrier, inc=1, device_id=target, device_id_type=MESH)

    pl.when(place.has_up)(lambda: signal({"expert": place.up}))
    pl.when(place.has_down)(lambda: signal({"expert": place.down}))
    signal({"expert": place.across})
    signal({"expert": place.sibling})
    count = 2 + place.has_up.astype(jnp.int32) + place.has_down.astype(jnp.int32)
    dps = lax.axis_size("dp")
    for step in range(1, dps):
        signal({"dp": lax.rem(lax.axis_index("dp") + step, dps)})
    count = count + (dps - 1)
    pl.semaphore_wait(barrier, count)


class Gather:
    def __init__(self, place, pieces, extra, send, recv):
        self.place, self.pieces, self.extra, self.send, self.recv = place, pieces, extra, send, recv

    def copy(self, piece, block, link):
        place = self.place
        view = self.extra(block) if piece is None else self.pieces(block, piece)
        number = PIECES if piece is None else piece
        target = {
            UP: {"expert": place.up},
            DOWN: {"expert": place.down},
            ACROSS: {"expert": place.across},
            SIBLING: {"expert": place.sibling},
            PARTNER: {"dp": place.partner},
        }[link]
        return pltpu.make_async_remote_copy(
            src_ref=view,
            dst_ref=view,
            send_sem=self.send.at[number, link, block],
            recv_sem=self.recv.at[number, block],
            device_id=target,
            device_id_type=MESH,
        )

    def arrive(self, piece, block):
        self.copy(piece, block, SIBLING).wait_recv()

    def mine(self, z):
        return self.place.at(z, self.place.x, self.place.core)

    def other(self, z):
        return self.place.at(z, 1 - self.place.x, self.place.core)

    def line_pieces(self):
        found = [] if self.extra is None else [(None, True)]
        for k in range(PIECES // 2):
            found += [(2 * k + self.place.parity, True), (2 * k + 1 - self.place.parity, False)]
        return found

    def begin(self, piece, shared):
        place, me = self.place, self.place.me
        pl.when(place.has_up)(lambda: self.copy(piece, me, UP).start())
        pl.when(place.has_down)(lambda: self.copy(piece, me, DOWN).start())
        if shared:
            self.copy(piece, me, ACROSS).start()
        self.copy(piece, me, SIBLING).start()

    def line_step(self, d, piece, shared):
        place = self.place
        for (z, there), onward, open_ in zip(
            place.by_distance(d), (UP, DOWN), (place.has_up, place.has_down)
        ):

            def body(z=z, onward=onward, open_=open_):
                self.arrive(piece, self.mine(z))
                pl.when(open_)(lambda: self.copy(piece, self.mine(z), onward).start())
                if shared:
                    self.copy(piece, self.mine(z), ACROSS).start()
                self.copy(piece, self.mine(z), SIBLING).start()

            when(there, body)

    def across_step(self, d, piece, shared):
        for z, there in self.place.by_distance(d):

            def body(z=z):
                self.arrive(piece, self.other(z))
                if shared and piece is not None:
                    self.copy(piece, self.other(z), PARTNER).start()
                self.copy(piece, self.other(z), SIBLING).start()

            when(there, body)

    def run(self):
        height = self.place.height
        for d in range(1, height + 2):
            for piece, shared in self.line_pieces():
                if d < height:
                    self.line_step(d, piece, shared)
                if shared and d <= height:
                    self.across_step(d - 1, piece, True)
                if not shared and d >= 2:
                    self.across_step(d - 2, piece, False)
        self.finish()

    def finish(self):
        place = self.place
        for z in range(place.height):
            for piece, shared in self.line_pieces():
                for x in range(COLUMNS):
                    self.arrive(piece, place.at(z, x, 1 - place.core))
                self.copy(piece, self.mine(z), SIBLING).wait_send()
                self.copy(piece, self.other(z), SIBLING).wait_send()
                if shared:
                    self.copy(piece, self.mine(z), ACROSS).wait_send()
                    if piece is not None:
                        self.copy(piece, self.other(z), PARTNER).wait_send()
                pl.when(jnp.logical_and(place.has_up, z <= place.z))(
                    lambda: self.copy(piece, self.mine(z), UP).wait_send()
                )
                pl.when(jnp.logical_and(place.has_down, z >= place.z))(
                    lambda: self.copy(piece, self.mine(z), DOWN).wait_send()
                )


def scatter(place, part_ref, bufs, sems, leave):
    core_in, partner_in, across_in, line_in, dp_in = bufs
    core_sems, partner_sems, across_sems, line_sems, dp_sems = [
        (sems[2 * i], sems[2 * i + 1]) for i in range(5)
    ]
    height = place.height
    rows = part_ref.shape[1] // PIECES
    dps = lax.axis_size("dp")
    dp = lax.axis_index("dp")
    f32 = jnp.float32

    def span_of(h):
        return pl.ds(pl.multiple_of(h * rows, rows), rows)

    def remote(source, target, pair, source_index, target_index, h, device):
        return pltpu.make_async_remote_copy(
            src_ref=source.at[source_index, span_of(h)],
            dst_ref=target.at[target_index, span_of(h)],
            send_sem=pair[0].at[source_index, h],
            recv_sem=pair[1].at[target_index, h],
            device_id=device,
            device_id_type=MESH,
        )

    def core_copy(z, x, h):
        spot = z * COLUMNS + x
        return pltpu.make_async_remote_copy(
            src_ref=part_ref.at[place.at(z, x, 1 - place.core), span_of(h)],
            dst_ref=core_in.at[spot, span_of(h)],
            send_sem=core_sems[0].at[spot, h],
            recv_sem=core_sems[1].at[spot, h],
            device_id={"expert": place.sibling},
            device_id_type=MESH,
        )

    def spot_of(z, x):
        return z * COLUMNS + x

    def partner_copy(z, h):
        return remote(
            core_in, partner_in, partner_sems, spot_of(z, 1 - place.x), z, h, {"dp": place.partner}
        )

    def across_copy(z, h):
        return remote(
            core_in, across_in, across_sems, spot_of(z, 1 - place.x), z, h, {"expert": place.across}
        )

    def line_copy(z, slot, h, target):
        return remote(
            core_in, line_in, line_sems, spot_of(z, place.x), slot, h, {"expert": target}
        )

    def line_arrive(slot, h):
        line_copy(0, slot, h, place.up).wait_recv()

    def dp_copy(step, h):
        return pltpu.make_async_remote_copy(
            src_ref=dp_in.at[dp, span_of(h)],
            dst_ref=dp_in.at[dp, span_of(h)],
            send_sem=dp_sems[0].at[step, h],
            recv_sem=dp_sems[1].at[dp, h],
            device_id={"dp": lax.rem(dp + step, dps)},
            device_id_type=MESH,
        )

    def dp_arrive(index, h):
        pltpu.make_async_remote_copy(
            src_ref=dp_in.at[dp, span_of(h)],
            dst_ref=dp_in.at[index, span_of(h)],
            send_sem=dp_sems[0].at[1, h],
            recv_sem=dp_sems[1].at[index, h],
            device_id={"dp": lax.rem(dp + 1, dps)},
            device_id_type=MESH,
        ).wait_recv()

    own_half = [2 * k + place.parity for k in range(PIECES // 2)]
    their_half = [2 * k + 1 - place.parity for k in range(PIECES // 2)]

    def planes(d, halves, body):
        for way, (z, there) in enumerate(place.by_distance(d)):
            for h, shared in halves:
                when(there, lambda z=z, h=h: body(z, h, shared, None if d == 0 else (DOWN, UP)[way]))

    both_halves = [(h, True) for h in own_half] + [(h, False) for h in their_half]

    def send_core(z, h, shared, way):
        core_copy(z, 1 - place.x, h).start()

    def send_core_own(z, h, shared, way):
        core_copy(z, place.x, h).start()

    def add_core(z, x, h):
        total = part_ref[place.at(z, x, place.core), span_of(h)].astype(f32)
        return total + core_in[spot_of(z, x), span_of(h)].astype(f32)

    def send_partner(z, h, shared, way):
        core_copy(z, 1 - place.x, h).wait_recv()
        core_in[spot_of(z, 1 - place.x), span_of(h)] = add_core(z, 1 - place.x, h).astype(jnp.bfloat16)
        partner_copy(z, h).start()

    def send_across(z, h, shared, way):
        core_copy(z, 1 - place.x, h).wait_recv()
        partner_copy(z, h).wait_recv()
        total = add_core(z, 1 - place.x, h) + partner_in[z, span_of(h)].astype(f32)
        core_in[spot_of(z, 1 - place.x), span_of(h)] = total.astype(jnp.bfloat16)
        across_copy(z, h).start()

    def send_line(z, h, shared, way):
        span = span_of(h)
        core_copy(z, place.x, h).wait_recv()
        if shared:
            across_copy(z, h).wait_recv()

        def total():
            own = add_core(z, place.x, h)
            return own + across_in[z, span].astype(f32) if shared else own

        if way is None:

            def store(value):
                dp_in[dp, span] = value.astype(jnp.bfloat16)

            def both():
                line_arrive(z, h)
                line_arrive(height, h)
                store(total() + line_in[z, span].astype(f32) + line_in[height, span].astype(f32))

            def above():
                line_arrive(z, h)
                store(total() + line_in[z, span].astype(f32))

            def below():
                line_arrive(height, h)
                store(total() + line_in[height, span].astype(f32))

            pl.when(jnp.logical_and(place.has_up, place.has_down))(both)
            pl.when(jnp.logical_and(place.has_up, jnp.logical_not(place.has_down)))(above)
            pl.when(jnp.logical_and(jnp.logical_not(place.has_up), place.has_down))(below)
            for step in range(1, dps):
                dp_copy(step, h).start()
            return
        if way == DOWN:
            before, slot, target = place.has_up, z, place.down
        else:
            before, target = place.has_down, place.up
            slot = jnp.where(z == place.z + 1, height, z)

        def store_line(value):
            core_in[spot_of(z, place.x), span] = value.astype(jnp.bfloat16)

        def with_arrival():
            line_arrive(z, h)
            store_line(total() + line_in[z, span].astype(f32))

        pl.when(before)(with_arrival)
        pl.when(jnp.logical_not(before))(lambda: store_line(total()))
        line_copy(z, slot, h, target).start()

    far_first = range(height - 1, -1, -1)
    for d in far_first:
        planes(d, both_halves[::-1], send_core)
    for d in far_first:
        planes(d, both_halves, send_core_own)
    for d in far_first:
        planes(d, both_halves[PIECES // 2 :], send_partner)
    for d in far_first:
        planes(d, both_halves[: PIECES // 2], send_across)
        if d + 1 < height:
            planes(d + 1, both_halves[::-1], send_line)
    planes(0, both_halves[::-1], send_line)

    for h, shared in both_halves[::-1]:
        for step in range(1, dps):
            dp_arrive(lax.rem(dp + step, dps), h)
        total = dp_in[0, span_of(h)].astype(f32)
        for index in range(1, dps):
            total = total + dp_in[index, span_of(h)].astype(f32)
        leave(h, shared, span_of(h), total)

    def settle(z, h, shared, way):
        core_copy(z, 0, h).wait_send()
        core_copy(z, 1, h).wait_send()
        (across_copy if shared else partner_copy)(z, h).wait_send()
        if way is not None:
            line_copy(z, 0, h, place.up).wait_send()

    def finish():
        for d in far_first:
            planes(d, both_halves, settle)
        for h in range(PIECES):
            for step in range(1, dps):
                dp_copy(step, h).wait_send()

    return finish


def scatter_scratch(n, rows, width):
    height = n // (CORES * COLUMNS)
    dps = lax.axis_size("dp")
    sizes = [height * COLUMNS, height, height, height + 1, dps]
    return (
        [pltpu.VMEM((size, rows, width), jnp.bfloat16) for size in sizes],
        [pltpu.SemaphoreType.DMA((count, PIECES)) for size in sizes for count in (max(sizes), size)],
    )


def gather_scratch(n):
    return [pltpu.SemaphoreType.DMA((PIECES + 1, 5, n)), pltpu.SemaphoreType.DMA((PIECES + 1, n))]


def token_pieces(ref):
    rows = ref.shape[1] // PIECES
    return lambda block, h: ref.at[block, pl.ds(pl.multiple_of(h * rows, rows), rows)]


def spread_kernel(n, tokens_ref, table_ref, rows_ref, tables_ref, send, recv):
    place = Place(n)
    rows_ref[place.me] = tokens_ref[...]
    tables_ref[place.me] = table_ref[...]
    greet(place)
    spread = Gather(place, token_pieces(rows_ref), lambda block: tables_ref.at[block], send, recv)
    for piece, shared in spread.line_pieces():
        spread.begin(piece, shared)
    spread.run()


def loss_kernel(n, part_ref, targets_ref, scales_ref, grads_ref, *scratch):
    place = Place(n)
    bufs, sems, (send, recv) = scratch[:5], scratch[5:15], scratch[15:]
    greet(place)
    spread = Gather(place, token_pieces(grads_ref), None, send, recv)

    def leave(h, shared, span, total):
        error = total - targets_ref[span, :].astype(jnp.float32)
        grads_ref[place.me, span] = (scales_ref[span, :] * error).astype(jnp.bfloat16)
        spread.begin(h, shared)

    finish = scatter(place, part_ref, bufs, sems, leave)
    spread.run()
    finish()


def return_kernel(n, part_ref, out_ref, *scratch):
    place = Place(n)
    bufs, sems = scratch[:5], scratch[5:15]
    greet(place)

    def leave(h, shared, span, total):
        out_ref[span, :] = total.astype(jnp.bfloat16)

    scatter(place, part_ref, bufs, sems, leave)()


def run(kernel, out_shape, scratch, number, *operands):
    single = not isinstance(out_shape, (list, tuple))
    whole = pl.BlockSpec(memory_space=pltpu.VMEM)
    return pl.pallas_call(
        kernel,
        out_shape=out_shape,
        in_specs=[whole] * len(operands),
        out_specs=whole if single else [whole] * len(out_shape),
        scratch_shapes=scratch,
        compiler_params=pltpu.CompilerParams(
            collective_id=number, has_side_effects=True, vmem_limit_bytes=60 * 2**20
        ),
    )(*operands)


def table_of(routes, route_gates, experts):
    count = routes.shape[0]
    hits = routes[None, :, :] == jnp.arange(experts, dtype=jnp.int32)[:, None, None]
    chosen = jnp.any(hits, 2)
    earlier = jnp.arange(count)[:, None] < jnp.arange(count)[None, :]
    places = jnp.dot(
        chosen.astype(jnp.bfloat16), earlier.astype(jnp.bfloat16), preferred_element_type=jnp.float32
    )
    places = jnp.where(chosen, places, -1.0)
    gates = jnp.sum(jnp.where(hits, route_gates.astype(jnp.float32)[None], 0.0), 2)
    return jnp.concatenate([places, gates], 0).astype(jnp.bfloat16)


def block_dot(left, right, contract):
    return lax.dot_general(
        left, right, ((contract[0], contract[1]), ((0,), (0,))), preferred_element_type=jnp.float32
    ).astype(jnp.bfloat16)


def shards(tokens, routes, route_gates, domains, domain_weight, targets, w_gate, w_up, w_down):
    count, width = tokens.shape
    n = lax.axis_size("expert")
    capacity = max(2, 4 * count * routes.shape[1] // (3 * n))
    bf16, f32 = jnp.bfloat16, jnp.float32
    contract_last = (((1,), (1,)), ((), ()))
    contract_first = (((0,), (0,)), ((), ()))

    table = table_of(routes, route_gates, n)
    rows, tables = run(
        functools.partial(spread_kernel, n),
        [jax.ShapeDtypeStruct((n, count, width), bf16), jax.ShapeDtypeStruct((n, 2 * n, count), bf16)],
        gather_scratch(n),
        0,
        tokens,
        table,
    )
    me = lax.axis_index("expert")
    places = lax.dynamic_index_in_dim(tables, me, 1, keepdims=True)
    gates = lax.dynamic_index_in_dim(tables, me + n, 1, keepdims=True)
    matches = places.astype(jnp.int32) == jnp.arange(capacity, dtype=jnp.int32)[None, :, None]
    select = matches.astype(bf16)
    gated = jnp.where(matches, gates, jnp.zeros((), bf16))

    slot_rows = block_dot(select, rows, ((2,), (1,))).reshape(n * capacity, width)
    gate_pre = jnp.dot(slot_rows, w_gate[0], preferred_element_type=f32)
    up_pre = jnp.dot(slot_rows, w_up[0], preferred_element_type=f32)
    hidden = (jax.nn.silu(gate_pre) * up_pre).astype(bf16)
    part = jnp.dot(hidden, w_down[0], preferred_element_type=f32).astype(bf16)
    outs = block_dot(gated, part.reshape(n, capacity, width), ((1,), (1,)))

    picks = domains[:, None] == jnp.arange(domain_weight.shape[0], dtype=jnp.int32)[None, :]
    scales = jnp.sum(jnp.where(picks, domain_weight[None, :], 0.0), 1, keepdims=True)
    bufs, sems = scatter_scratch(n, count, width)
    loss_grads = run(
        functools.partial(loss_kernel, n),
        jax.ShapeDtypeStruct((n, count, width), bf16),
        bufs + sems + gather_scratch(n),
        1,
        outs,
        targets,
        scales,
    )

    slot_grads = block_dot(gated, loss_grads, ((2,), (1,))).reshape(n * capacity, width)
    hidden_grad = lax.dot_general(slot_grads, w_down[0], contract_last, preferred_element_type=f32)
    sigma = jax.nn.sigmoid(gate_pre)
    gate_grad = (hidden_grad * up_pre * sigma * (1.0 + gate_pre * (1.0 - sigma))).astype(bf16)
    up_grad = (hidden_grad * gate_pre * sigma).astype(bf16)
    row_part = lax.dot_general(gate_grad, w_gate[0], contract_last, preferred_element_type=f32)
    row_part = row_part + lax.dot_general(up_grad, w_up[0], contract_last, preferred_element_type=f32)
    backs = block_dot(select, row_part.astype(bf16).reshape(n, capacity, width), ((1,), (1,)))
    grad_tokens = run(
        functools.partial(return_kernel, n),
        jax.ShapeDtypeStruct((count, width), bf16),
        bufs + sems,
        2,
        backs,
    )
    grad_down = lax.dot_general(hidden, slot_grads, contract_first, preferred_element_type=f32)
    grad_gate = lax.dot_general(slot_rows, gate_grad, contract_first, preferred_element_type=f32)
    grad_up = lax.dot_general(slot_rows, up_grad, contract_first, preferred_element_type=f32)
    return grad_tokens, grad_gate[None], grad_up[None], grad_down[None]


def solution(mesh):
    return jax.shard_map(
        shards,
        mesh=mesh,
        in_specs=(
            P("expert", None),
            P("expert", None),
            P("expert", None),
            P("expert"),
            P(),
            P("expert", None),
            P("expert", None, "dp"),
            P("expert", None, "dp"),
            P("expert", "dp", None),
        ),
        out_specs=(
            P("expert", None),
            P("expert", None, "dp"),
            P("expert", None, "dp"),
            P("expert", "dp", None),
        ),
        check_vma=False,
    )
```

```python
import functools

import jax
import jax.numpy as jnp
from jax import lax
from jax.experimental import pallas as pl
from jax.experimental.pallas import tpu as pltpu
from jax.sharding import PartitionSpec as P

MESH = pl.DeviceIdType.MESH
CORES = 2
COLUMNS = 2
HALVES = 2
LAG = 4
UP, DOWN, ACROSS, SIBLING = range(4)


class Place:
    def __init__(self, n):
        self.n = n
        self.height = n // (CORES * COLUMNS)
        self.me = lax.axis_index("expert")
        self.core = lax.rem(self.me, CORES)
        self.x = lax.rem(self.me // CORES, COLUMNS)
        self.z = self.me // (CORES * COLUMNS)
        self.up = self.me + CORES * COLUMNS
        self.down = self.me - CORES * COLUMNS
        self.has_up = self.z + 1 < self.height
        self.has_down = self.z > 0
        self.across = self.at(self.z, 1 - self.x, self.core)
        self.sibling = self.at(self.z, self.x, 1 - self.core)

    def at(self, z, x, core):
        return (z * COLUMNS + x) * CORES + core

    def by_distance(self, d):
        if d == 0:
            return [(self.z, None)]
        return [(self.z - d, self.z - d >= 0), (self.z + d, self.z + d < self.height)]


def when(condition, body):
    if condition is None:
        body()
    else:
        pl.when(condition)(body)


def greet(place):
    barrier = pltpu.get_barrier_semaphore()

    def signal(target):
        pl.semaphore_signal(barrier, inc=1, device_id=target, device_id_type=MESH)

    pl.when(place.has_up)(lambda: signal({"expert": place.up}))
    pl.when(place.has_down)(lambda: signal({"expert": place.down}))
    signal({"expert": place.across})
    signal({"expert": place.sibling})
    count = 2 + place.has_up.astype(jnp.int32) + place.has_down.astype(jnp.int32)
    dps = lax.axis_size("dp")
    for step in range(1, dps):
        signal({"dp": lax.rem(lax.axis_index("dp") + step, dps)})
    count = count + (dps - 1)
    pl.semaphore_wait(barrier, count)


class Gather:
    def __init__(self, place, pieces, send, recv):
        self.place, self.pieces, self.send, self.recv = place, pieces, send, recv

    def copy(self, piece, block, link):
        place = self.place
        view = self.pieces[piece](block)
        target = (place.up, place.down, place.across, place.sibling)[link]
        return pltpu.make_async_remote_copy(
            src_ref=view,
            dst_ref=view,
            send_sem=self.send.at[piece, link, block],
            recv_sem=self.recv.at[piece, block],
            device_id={"expert": target},
            device_id_type=MESH,
        )

    def arrive(self, piece, block):
        self.copy(piece, block, SIBLING).wait_recv()

    def mine(self, z):
        return self.place.at(z, self.place.x, self.place.core)

    def other(self, z):
        return self.place.at(z, 1 - self.place.x, self.place.core)

    def begin(self, piece):
        place, me = self.place, self.place.me
        pl.when(place.has_up)(lambda: self.copy(piece, me, UP).start())
        pl.when(place.has_down)(lambda: self.copy(piece, me, DOWN).start())
        self.copy(piece, me, ACROSS).start()
        self.copy(piece, me, SIBLING).start()

    def line_step(self, d, piece):
        place = self.place
        for (z, there), onward, open_ in zip(
            place.by_distance(d), (UP, DOWN), (place.has_up, place.has_down)
        ):

            def body(z=z, onward=onward, open_=open_):
                self.arrive(piece, self.mine(z))
                pl.when(open_)(lambda: self.copy(piece, self.mine(z), onward).start())
                self.copy(piece, self.mine(z), ACROSS).start()
                self.copy(piece, self.mine(z), SIBLING).start()

            when(there, body)

    def across_step(self, d, piece):
        for z, there in self.place.by_distance(d):

            def body(z=z):
                self.arrive(piece, self.other(z))
                self.copy(piece, self.other(z), SIBLING).start()

            when(there, body)

    def from_sibling(self, z):
        for piece in range(len(self.pieces)):
            for x in range(COLUMNS):
                self.arrive(piece, self.place.at(z, x, 1 - self.place.core))

    def steps(self, piece):
        height = self.place.height
        found = []
        for d in range(1, height):
            found.append(lambda d=d: self.line_step(d, piece))
            found.append(lambda d=d: self.across_step(d - 1, piece))
        found.append(lambda: self.across_step(height - 1, piece))
        return found

    def settle(self):
        place = self.place
        for z in range(place.height):
            for piece in range(len(self.pieces)):
                self.copy(piece, self.mine(z), ACROSS).wait_send()
                self.copy(piece, self.mine(z), SIBLING).wait_send()
                self.copy(piece, self.other(z), SIBLING).wait_send()
                pl.when(jnp.logical_and(place.has_up, z <= place.z))(
                    lambda: self.copy(piece, self.mine(z), UP).wait_send()
                )
                pl.when(jnp.logical_and(place.has_down, z >= place.z))(
                    lambda: self.copy(piece, self.mine(z), DOWN).wait_send()
                )


def staggered(first, second, lag):
    for i in range(max(len(first), len(second) + lag)):
        if i < len(first):
            first[i]()
        if i >= lag and i - lag < len(second):
            second[i - lag]()


def scatter(place, part_ref, bufs, sems, leave):
    core_in, across_out, across_in, line_out, line_in, dp_in = bufs
    core_send, core_recv, across_send, across_recv, line_send, line_recv, dp_send, dp_recv = sems
    height = place.height
    rows = part_ref.shape[1] // HALVES
    dps = lax.axis_size("dp")
    dp = lax.axis_index("dp")
    spans = [pl.ds(h * rows, rows) for h in range(HALVES)]
    f32 = jnp.float32

    def core_copy(z, x, h):
        spot = z * COLUMNS + x
        return pltpu.make_async_remote_copy(
            src_ref=part_ref.at[place.at(z, x, 1 - place.core), spans[h]],
            dst_ref=core_in.at[spot, spans[h]],
            send_sem=core_send.at[spot, h],
            recv_sem=core_recv.at[spot, h],
            device_id={"expert": place.sibling},
            device_id_type=MESH,
        )

    def across_copy(z, h):
        return pltpu.make_async_remote_copy(
            src_ref=across_out.at[z, spans[h]],
            dst_ref=across_in.at[z, spans[h]],
            send_sem=across_send.at[z, h],
            recv_sem=across_recv.at[z, h],
            device_id={"expert": place.across},
            device_id_type=MESH,
        )

    def line_copy(z, slot, h, target):
        return pltpu.make_async_remote_copy(
            src_ref=line_out.at[z, spans[h]],
            dst_ref=line_in.at[slot, spans[h]],
            send_sem=line_send.at[z, h],
            recv_sem=line_recv.at[slot, h],
            device_id={"expert": target},
            device_id_type=MESH,
        )

    def line_arrive(slot, h):
        line_copy(0, slot, h, place.up).wait_recv()

    def dp_copy(step, h):
        return pltpu.make_async_remote_copy(
            src_ref=dp_in.at[dp, spans[h]],
            dst_ref=dp_in.at[dp, spans[h]],
            send_sem=dp_send.at[step, h],
            recv_sem=dp_recv.at[dp, h],
            device_id={"dp": lax.rem(dp + step, dps)},
            device_id_type=MESH,
        )

    def dp_arrive(index, h):
        pltpu.make_async_remote_copy(
            src_ref=dp_in.at[dp, spans[h]],
            dst_ref=dp_in.at[index, spans[h]],
            send_sem=dp_send.at[1, h],
            recv_sem=dp_recv.at[index, h],
            device_id={"dp": lax.rem(dp + 1, dps)},
            device_id_type=MESH,
        ).wait_recv()

    def planes(d, h, body):
        for way, (z, there) in enumerate(place.by_distance(d)):
            when(there, lambda z=z: body(z, h, None if d == 0 else (DOWN, UP)[way]))

    def send_core(z, h, way):
        core_copy(z, 1 - place.x, h).start()

    def send_core_own(z, h, way):
        core_copy(z, place.x, h).start()

    def send_across(z, h, way):
        core_copy(z, 1 - place.x, h).wait_recv()
        span = spans[h]
        total = part_ref[place.at(z, 1 - place.x, place.core), span].astype(f32)
        total = total + core_in[z * COLUMNS + 1 - place.x, span].astype(f32)
        across_out[z, span] = total.astype(jnp.bfloat16)
        across_copy(z, h).start()

    def send_line(z, h, way):
        span = spans[h]
        core_copy(z, place.x, h).wait_recv()
        across_copy(z, h).wait_recv()

        def total():
            own = part_ref[place.at(z, place.x, place.core), span].astype(f32)
            own = own + core_in[z * COLUMNS + place.x, span].astype(f32)
            return own + across_in[z, span].astype(f32)

        if way is None:

            def store(value):
                dp_in[dp, span] = value.astype(jnp.bfloat16)

            def both():
                line_arrive(z, h)
                line_arrive(height, h)
                store(total() + line_in[z, span].astype(f32) + line_in[height, span].astype(f32))

            def above():
                line_arrive(z, h)
                store(total() + line_in[z, span].astype(f32))

            def below():
                line_arrive(height, h)
                store(total() + line_in[height, span].astype(f32))

            pl.when(jnp.logical_and(place.has_up, place.has_down))(both)
            pl.when(jnp.logical_and(place.has_up, jnp.logical_not(place.has_down)))(above)
            pl.when(jnp.logical_and(jnp.logical_not(place.has_up), place.has_down))(below)
            for step in range(1, dps):
                dp_copy(step, h).start()
            return
        if way == DOWN:
            before, slot, target = place.has_up, z, place.down
        else:
            before, target = place.has_down, place.up
            slot = jnp.where(z == place.z + 1, height, z)

        def with_arrival():
            line_arrive(z, h)
            line_out[z, span] = (total() + line_in[z, span].astype(f32)).astype(jnp.bfloat16)

        def alone():
            line_out[z, span] = total().astype(jnp.bfloat16)

        pl.when(before)(with_arrival)
        pl.when(jnp.logical_not(before))(alone)
        line_copy(z, slot, h, target).start()

    far_first = list(range(height - 1, -1, -1))

    def begin():
        for h in range(HALVES):
            for body in (send_core, send_core_own):
                for d in far_first:
                    planes(d, h, body)

    def last(h):
        for step in range(1, dps):
            dp_arrive(lax.rem(dp + step, dps), h)
        total = dp_in[0, spans[h]].astype(f32)
        for index in range(1, dps):
            total = total + dp_in[index, spans[h]].astype(f32)
        leave(h, spans[h], total)

    def steps(h):
        found = []
        for d in far_first:
            found.append(lambda d=d: planes(d, h, send_across))
            if d + 1 < height:
                found.append(lambda d=d: planes(d + 1, h, send_line))
        found.append(lambda: planes(0, h, send_line))
        found.append(lambda: last(h))
        return found

    def settle(z, h, way):
        core_copy(z, 0, h).wait_send()
        core_copy(z, 1, h).wait_send()
        across_copy(z, h).wait_send()
        if way is not None:
            line_copy(z, 0, h, place.up).wait_send()

    def finish():
        for h in range(HALVES):
            for d in far_first:
                planes(d, h, settle)
            for step in range(1, dps):
                dp_copy(step, h).wait_send()

    return begin, steps, finish


def scatter_scratch(n, rows, width):
    height = n // (CORES * COLUMNS)
    dps = lax.axis_size("dp")
    sizes = [height * COLUMNS, height, height, height, height + 1, dps]
    sems = [height * COLUMNS] * 2 + [height] * 3 + [height + 1] + [dps] * 2
    return (
        [pltpu.VMEM((size, rows, width), jnp.bfloat16) for size in sizes],
        [pltpu.SemaphoreType.DMA((size, HALVES)) for size in sems],
    )


def gather_scratch(n, pieces):
    return [pltpu.SemaphoreType.DMA((pieces, 4, n)), pltpu.SemaphoreType.DMA((pieces, n))]


def token_pieces(ref):
    rows = ref.shape[1] // HALVES
    return [lambda block, h=h: ref.at[block, pl.ds(h * rows, rows)] for h in range(HALVES)]


def forward_kernel(
    n,
    capacity,
    tokens_ref,
    table_ref,
    w_gate_ref,
    w_up_ref,
    w_down_ref,
    tables_ref,
    slot_rows_out,
    gate_out,
    up_out,
    hidden_out,
    outs_out,
    rows_ref,
    slot_rows_ref,
    gate_ref,
    up_ref,
    hidden_ref,
    outs_ref,
    send,
    recv,
    leaving,
):
    place = Place(n)
    group = CORES * COLUMNS
    bf16, f32 = jnp.bfloat16, jnp.float32
    rows_ref[place.me] = tokens_ref[...]
    tables_ref[place.me] = table_ref[...]
    greet(place)
    pieces = [lambda block: tables_ref.at[block]] + token_pieces(rows_ref)
    spread = Gather(place, pieces, send, recv)
    results = [
        (slot_rows_ref, slot_rows_out),
        (gate_ref, gate_out),
        (up_ref, up_out),
        (hidden_ref, hidden_out),
        (outs_ref, outs_out),
    ]

    def copies_out(z):
        return [
            pltpu.make_async_copy(source.at[z], target.at[z], leaving.at[i, z])
            for i, (source, target) in enumerate(results)
        ]

    def matches(block):
        places = tables_ref[block, pl.ds(place.me, 1), :]
        spots = lax.broadcasted_iota(jnp.int32, (capacity, places.shape[1]), 0).astype(f32)
        return places == spots

    def compute(z):
        spread.from_sibling(z)
        for i in range(group):
            block = z * group + i
            select = jnp.where(matches(block), 1.0, 0.0).astype(bf16)
            slot_rows_ref[z, pl.ds(i * capacity, capacity)] = jnp.dot(
                select, rows_ref[block], preferred_element_type=f32
            ).astype(bf16)
        gate_pre = jnp.dot(slot_rows_ref[z], w_gate_ref[0], preferred_element_type=f32)
        up_pre = jnp.dot(slot_rows_ref[z], w_up_ref[0], preferred_element_type=f32)
        gate_ref[z] = gate_pre
        up_ref[z] = up_pre
        hidden = (gate_pre * jax.nn.sigmoid(gate_pre) * up_pre).astype(bf16)
        hidden_ref[z] = hidden
        part = jnp.dot(hidden, w_down_ref[0], preferred_element_type=f32).astype(bf16)
        for i in range(group):
            block = z * group + i
            gates = tables_ref[block, pl.ds(place.me + n, 1), :]
            gated = jnp.where(matches(block), gates, 0.0).astype(bf16)
            outs_ref[z, i] = lax.dot_general(
                gated,
                part[i * capacity : (i + 1) * capacity],
                (((0,), (0,)), ((), ())),
                preferred_element_type=f32,
            ).astype(bf16)
        for copy in copies_out(z):
            copy.start()

    def compute_at(d):
        if d == 0:
            compute(place.z)
            return

        @pl.loop(0, 2)
        def _(side):
            z = place.z + (2 * side - 1) * d
            pl.when(jnp.logical_and(z >= 0, z < place.height))(lambda: compute(z))

    for piece in range(len(pieces)):
        spread.begin(piece)
    for d in range(1, place.height + 1):
        for piece in range(len(pieces)):
            if d < place.height:
                spread.line_step(d, piece)
            spread.across_step(d - 1, piece)
        compute_at(d - 1)
    spread.settle()
    for z in range(place.height):
        for copy in copies_out(z):
            copy.wait()


def loss_kernel(n, part_ref, targets_ref, scales_ref, grads_ref, *scratch):
    place = Place(n)
    bufs, sems, (send, recv) = scratch[:6], scratch[6:14], scratch[14:]
    greet(place)
    spread = Gather(place, token_pieces(grads_ref), send, recv)

    def leave(h, span, total):
        error = total - targets_ref[span, :].astype(jnp.float32)
        grads_ref[place.me, span] = (scales_ref[span, :] * error).astype(jnp.bfloat16)
        spread.begin(h)

    begin, steps, finish = scatter(place, part_ref, bufs, sems, leave)
    begin()
    staggered(steps(0) + spread.steps(0), steps(1) + spread.steps(1), LAG)
    for z in range(place.height):
        spread.from_sibling(z)
    spread.settle()
    finish()


def return_kernel(n, part_ref, out_ref, *scratch):
    place = Place(n)
    bufs, sems = scratch[:6], scratch[6:14]
    greet(place)

    def leave(h, span, total):
        out_ref[span, :] = total.astype(jnp.bfloat16)

    begin, steps, finish = scatter(place, part_ref, bufs, sems, leave)
    begin()
    staggered(steps(0), steps(1), 1)
    finish()


def run(kernel, out_shape, scratch, number, *operands):
    single = not isinstance(out_shape, (list, tuple))
    whole = pl.BlockSpec(memory_space=pltpu.VMEM)
    outside = pl.BlockSpec(memory_space=pl.ANY)
    return pl.pallas_call(
        kernel,
        out_shape=out_shape,
        in_specs=[whole] * len(operands),
        out_specs=whole if single else [whole] + [outside] * (len(out_shape) - 1),
        scratch_shapes=scratch,
        compiler_params=pltpu.CompilerParams(
            collective_id=number, has_side_effects=True, vmem_limit_bytes=60 * 2**20
        ),
    )(*operands)


def table_of(routes, route_gates, experts):
    count = routes.shape[0]
    hits = routes[None, :, :] == jnp.arange(experts, dtype=jnp.int32)[:, None, None]
    chosen = jnp.any(hits, 2)
    earlier = jnp.arange(count)[:, None] < jnp.arange(count)[None, :]
    places = jnp.dot(
        chosen.astype(jnp.bfloat16), earlier.astype(jnp.bfloat16), preferred_element_type=jnp.float32
    )
    places = jnp.where(chosen, places, -1.0)
    gates = jnp.sum(jnp.where(hits, route_gates.astype(jnp.float32)[None], 0.0), 2)
    return jnp.concatenate([places, gates], 0)


def block_dot(left, right, contract):
    return lax.dot_general(
        left, right, ((contract[0], contract[1]), ((0,), (0,))), preferred_element_type=jnp.float32
    ).astype(jnp.bfloat16)


def shards(tokens, routes, route_gates, domains, domain_weight, targets, w_gate, w_up, w_down):
    count, width = tokens.shape
    n = lax.axis_size("expert")
    capacity = max(2, 4 * count * routes.shape[1] // (3 * n))
    bf16, f32 = jnp.bfloat16, jnp.float32
    contract_last = (((1,), (1,)), ((), ()))
    contract_first = (((0,), (0,)), ((), ()))

    table = table_of(routes, route_gates, n)
    height = n // (CORES * COLUMNS)
    slots = n * capacity // height
    hidden_width = w_gate.shape[2]
    shapes = [
        ((height, slots, width), bf16),
        ((height, slots, hidden_width), f32),
        ((height, slots, hidden_width), f32),
        ((height, slots, hidden_width), bf16),
        ((height, n // height, count, width), bf16),
    ]
    tables, slot_rows, gate_pre, up_pre, hidden, outs = run(
        functools.partial(forward_kernel, n, capacity),
        [jax.ShapeDtypeStruct((n, 2 * n, count), f32)]
        + [jax.ShapeDtypeStruct(*shape) for shape in shapes],
        [pltpu.VMEM((n, count, width), bf16)]
        + [pltpu.VMEM(*shape) for shape in shapes]
        + gather_scratch(n, HALVES + 1)
        + [pltpu.SemaphoreType.DMA((len(shapes), height))],
        0,
        tokens,
        table,
        w_gate,
        w_up,
        w_down,
    )
    slot_rows = slot_rows.reshape(n * capacity, width)
    gate_pre, up_pre, hidden = (
        item.reshape(n * capacity, hidden_width) for item in (gate_pre, up_pre, hidden)
    )
    outs = outs.reshape(n, count, width)
    me = lax.axis_index("expert")
    places = lax.dynamic_index_in_dim(tables, me, 1, keepdims=True)
    gates = lax.dynamic_index_in_dim(tables, me + n, 1, keepdims=True)
    matches = places == jnp.arange(capacity, dtype=f32)[None, :, None]
    select = matches.astype(bf16)
    gated = jnp.where(matches, gates, 0.0).astype(bf16)

    picks = domains[:, None] == jnp.arange(domain_weight.shape[0], dtype=jnp.int32)[None, :]
    scales = jnp.sum(jnp.where(picks, domain_weight[None, :], 0.0), 1, keepdims=True)
    bufs, sems = scatter_scratch(n, count, width)
    loss_grads = run(
        functools.partial(loss_kernel, n),
        jax.ShapeDtypeStruct((n, count, width), bf16),
        bufs + sems + gather_scratch(n, HALVES),
        1,
        outs,
        targets,
        scales,
    )

    slot_grads = block_dot(gated, loss_grads, ((2,), (1,))).reshape(n * capacity, width)
    hidden_grad = lax.dot_general(slot_grads, w_down[0], contract_last, preferred_element_type=f32)
    sigma = jax.nn.sigmoid(gate_pre)
    gate_grad = (hidden_grad * up_pre * sigma * (1.0 + gate_pre * (1.0 - sigma))).astype(bf16)
    up_grad = (hidden_grad * gate_pre * sigma).astype(bf16)
    row_part = lax.dot_general(gate_grad, w_gate[0], contract_last, preferred_element_type=f32)
    row_part = row_part + lax.dot_general(up_grad, w_up[0], contract_last, preferred_element_type=f32)
    backs = block_dot(select, row_part.astype(bf16).reshape(n, capacity, width), ((1,), (1,)))
    grad_tokens = run(
        functools.partial(return_kernel, n),
        jax.ShapeDtypeStruct((count, width), bf16),
        bufs + sems,
        2,
        backs,
    )
    grad_down = lax.dot_general(hidden, slot_grads, contract_first, preferred_element_type=f32)
    grad_gate = lax.dot_general(slot_rows, gate_grad, contract_first, preferred_element_type=f32)
    grad_up = lax.dot_general(slot_rows, up_grad, contract_first, preferred_element_type=f32)
    return grad_tokens, grad_gate[None], grad_up[None], grad_down[None]


def solution(mesh):
    return jax.shard_map(
        shards,
        mesh=mesh,
        in_specs=(
            P("expert", None),
            P("expert", None),
            P("expert", None),
            P("expert"),
            P(),
            P("expert", None),
            P("expert", None, "dp"),
            P("expert", None, "dp"),
            P("expert", "dp", None),
        ),
        out_specs=(
            P("expert", None),
            P("expert", None, "dp"),
            P("expert", None, "dp"),
            P("expert", "dp", None),
        ),
        check_vma=False,
    )
```

```python
import functools
import math

import jax
import jax.numpy as jnp
from jax import lax
from jax.experimental import pallas as pl
from jax.experimental.pallas import tpu as pltpu
from jax.sharding import PartitionSpec as P

MESH = pl.DeviceIdType.MESH
CORES = 2
COLUMNS = 2
HALVES = 2
UP, DOWN, ACROSS, SIBLING = range(4)


class Place:
    def __init__(self, n):
        self.n = n
        self.height = n // (CORES * COLUMNS)
        self.me = lax.axis_index("expert")
        self.core = lax.rem(self.me, CORES)
        self.x = lax.rem(self.me // CORES, COLUMNS)
        self.z = self.me // (CORES * COLUMNS)
        self.up = self.me + CORES * COLUMNS
        self.down = self.me - CORES * COLUMNS
        self.has_up = self.z + 1 < self.height
        self.has_down = self.z > 0
        self.across = self.at(self.z, 1 - self.x, self.core)
        self.sibling = self.at(self.z, self.x, 1 - self.core)

    def at(self, z, x, core):
        return (z * COLUMNS + x) * CORES + core

    def by_distance(self, d):
        if d == 0:
            return [(self.z, None)]
        return [(self.z - d, self.z - d >= 0), (self.z + d, self.z + d < self.height)]


def when(condition, body):
    if condition is None:
        body()
    else:
        pl.when(condition)(body)


def greet(place):
    barrier = pltpu.get_barrier_semaphore()

    def signal(target):
        pl.semaphore_signal(barrier, inc=1, device_id=target, device_id_type=MESH)

    pl.when(place.has_up)(lambda: signal({"expert": place.up}))
    pl.when(place.has_down)(lambda: signal({"expert": place.down}))
    signal({"expert": place.across})
    signal({"expert": place.sibling})
    count = 2 + place.has_up.astype(jnp.int32) + place.has_down.astype(jnp.int32)
    dps = lax.axis_size("dp")
    for step in range(1, dps):
        signal({"dp": lax.rem(lax.axis_index("dp") + step, dps)})
    count = count + (dps - 1)
    pl.semaphore_wait(barrier, count)


class Gather:
    def __init__(self, place, pieces, send, recv):
        self.place, self.pieces, self.send, self.recv = place, pieces, send, recv

    def copy(self, piece, block, link):
        place = self.place
        view = self.pieces[piece](block)
        target = (place.up, place.down, place.across, place.sibling)[link]
        return pltpu.make_async_remote_copy(
            src_ref=view,
            dst_ref=view,
            send_sem=self.send.at[piece, link, block],
            recv_sem=self.recv.at[piece, block],
            device_id={"expert": target},
            device_id_type=MESH,
        )

    def arrive(self, piece, block):
        self.copy(piece, block, SIBLING).wait_recv()

    def mine(self, z):
        return self.place.at(z, self.place.x, self.place.core)

    def other(self, z):
        return self.place.at(z, 1 - self.place.x, self.place.core)

    def begin(self, piece):
        place, me = self.place, self.place.me
        pl.when(place.has_up)(lambda: self.copy(piece, me, UP).start())
        pl.when(place.has_down)(lambda: self.copy(piece, me, DOWN).start())
        self.copy(piece, me, ACROSS).start()
        self.copy(piece, me, SIBLING).start()

    def line_step(self, d, piece):
        place = self.place
        for (z, there), onward, open_ in zip(
            place.by_distance(d), (UP, DOWN), (place.has_up, place.has_down)
        ):

            def body(z=z, onward=onward, open_=open_):
                self.arrive(piece, self.mine(z))
                pl.when(open_)(lambda: self.copy(piece, self.mine(z), onward).start())
                self.copy(piece, self.mine(z), ACROSS).start()
                self.copy(piece, self.mine(z), SIBLING).start()

            when(there, body)

    def across_step(self, d, piece):
        for z, there in self.place.by_distance(d):

            def body(z=z):
                self.arrive(piece, self.other(z))
                self.copy(piece, self.other(z), SIBLING).start()

            when(there, body)

    def from_sibling(self, z):
        for piece in range(len(self.pieces)):
            for x in range(COLUMNS):
                self.arrive(piece, self.place.at(z, x, 1 - self.place.core))

    def steps(self, piece):
        height = self.place.height
        found = []
        for d in range(1, height):
            found.append(lambda d=d: self.line_step(d, piece))
            found.append(lambda d=d: self.across_step(d - 1, piece))
        found.append(lambda: self.across_step(height - 1, piece))
        return found

    def run(self, compute, loads):
        place = self.place
        for d in range(1, place.height + 1):
            for piece in range(len(self.pieces)):
                if d < place.height:
                    self.line_step(d, piece)
                self.across_step(d - 1, piece)
            if d == 1:
                for copy in loads:
                    copy.wait()
                compute(place.z)
                continue

            @pl.loop(0, 2)
            def _(side, d=d):
                z = place.z + (2 * side - 1) * (d - 1)
                pl.when(jnp.logical_and(z >= 0, z < place.height))(lambda: compute(z))

        self.settle()

    def settle(self):
        place = self.place
        for z in range(place.height):
            for piece in range(len(self.pieces)):
                self.copy(piece, self.mine(z), ACROSS).wait_send()
                self.copy(piece, self.mine(z), SIBLING).wait_send()
                self.copy(piece, self.other(z), SIBLING).wait_send()
                pl.when(jnp.logical_and(place.has_up, z <= place.z))(
                    lambda: self.copy(piece, self.mine(z), UP).wait_send()
                )
                pl.when(jnp.logical_and(place.has_down, z >= place.z))(
                    lambda: self.copy(piece, self.mine(z), DOWN).wait_send()
                )


def staggered(first, second, lag):
    for i in range(max(len(first), len(second) + lag)):
        if i < len(first):
            first[i]()
        if i >= lag and i - lag < len(second):
            second[i - lag]()


def scatter(place, part_ref, bufs, sems, leave):
    core_in, across_out, across_in, line_out, line_in, dp_in = bufs
    core_send, core_recv, across_send, across_recv, line_send, line_recv, dp_send, dp_recv = sems
    height = place.height
    rows = part_ref.shape[1] // HALVES
    dps = lax.axis_size("dp")
    dp = lax.axis_index("dp")
    spans = [pl.ds(h * rows, rows) for h in range(HALVES)]
    f32 = jnp.float32

    def core_copy(z, x, h):
        spot = z * COLUMNS + x
        return pltpu.make_async_remote_copy(
            src_ref=part_ref.at[place.at(z, x, 1 - place.core), spans[h]],
            dst_ref=core_in.at[spot, spans[h]],
            send_sem=core_send.at[spot, h],
            recv_sem=core_recv.at[spot, h],
            device_id={"expert": place.sibling},
            device_id_type=MESH,
        )

    def across_copy(z, h):
        return pltpu.make_async_remote_copy(
            src_ref=across_out.at[z, spans[h]],
            dst_ref=across_in.at[z, spans[h]],
            send_sem=across_send.at[z, h],
            recv_sem=across_recv.at[z, h],
            device_id={"expert": place.across},
            device_id_type=MESH,
        )

    def line_copy(z, slot, h, target):
        return pltpu.make_async_remote_copy(
            src_ref=line_out.at[z, spans[h]],
            dst_ref=line_in.at[slot, spans[h]],
            send_sem=line_send.at[z, h],
            recv_sem=line_recv.at[slot, h],
            device_id={"expert": target},
            device_id_type=MESH,
        )

    def line_arrive(slot, h):
        line_copy(0, slot, h, place.up).wait_recv()

    def dp_copy(step, h):
        return pltpu.make_async_remote_copy(
            src_ref=dp_in.at[dp, spans[h]],
            dst_ref=dp_in.at[dp, spans[h]],
            send_sem=dp_send.at[step, h],
            recv_sem=dp_recv.at[dp, h],
            device_id={"dp": lax.rem(dp + step, dps)},
            device_id_type=MESH,
        )

    def dp_arrive(index, h):
        pltpu.make_async_remote_copy(
            src_ref=dp_in.at[dp, spans[h]],
            dst_ref=dp_in.at[index, spans[h]],
            send_sem=dp_send.at[1, h],
            recv_sem=dp_recv.at[index, h],
            device_id={"dp": lax.rem(dp + 1, dps)},
            device_id_type=MESH,
        ).wait_recv()

    def planes(d, h, body):
        for way, (z, there) in enumerate(place.by_distance(d)):
            when(there, lambda z=z: body(z, h, None if d == 0 else (DOWN, UP)[way]))

    def send_core(z, h, way):
        core_copy(z, 1 - place.x, h).start()

    def send_core_own(z, h, way):
        core_copy(z, place.x, h).start()

    def send_across(z, h, way):
        core_copy(z, 1 - place.x, h).wait_recv()
        span = spans[h]
        total = part_ref[place.at(z, 1 - place.x, place.core), span].astype(f32)
        total = total + core_in[z * COLUMNS + 1 - place.x, span].astype(f32)
        across_out[z, span] = total.astype(jnp.bfloat16)
        across_copy(z, h).start()

    def send_line(z, h, way):
        span = spans[h]
        core_copy(z, place.x, h).wait_recv()
        across_copy(z, h).wait_recv()

        def total():
            own = part_ref[place.at(z, place.x, place.core), span].astype(f32)
            own = own + core_in[z * COLUMNS + place.x, span].astype(f32)
            return own + across_in[z, span].astype(f32)

        if way is None:

            def store(value):
                dp_in[dp, span] = value.astype(jnp.bfloat16)

            def both():
                line_arrive(z, h)
                line_arrive(height, h)
                store(total() + line_in[z, span].astype(f32) + line_in[height, span].astype(f32))

            def above():
                line_arrive(z, h)
                store(total() + line_in[z, span].astype(f32))

            def below():
                line_arrive(height, h)
                store(total() + line_in[height, span].astype(f32))

            pl.when(jnp.logical_and(place.has_up, place.has_down))(both)
            pl.when(jnp.logical_and(place.has_up, jnp.logical_not(place.has_down)))(above)
            pl.when(jnp.logical_and(jnp.logical_not(place.has_up), place.has_down))(below)
            for step in range(1, dps):
                dp_copy(step, h).start()
            return
        if way == DOWN:
            before, slot, target = place.has_up, z, place.down
        else:
            before, target = place.has_down, place.up
            slot = jnp.where(z == place.z + 1, height, z)

        def with_arrival():
            line_arrive(z, h)
            line_out[z, span] = (total() + line_in[z, span].astype(f32)).astype(jnp.bfloat16)

        def alone():
            line_out[z, span] = total().astype(jnp.bfloat16)

        pl.when(before)(with_arrival)
        pl.when(jnp.logical_not(before))(alone)
        line_copy(z, slot, h, target).start()

    far_first = list(range(height - 1, -1, -1))

    def begin():
        for h in range(HALVES):
            for body in (send_core, send_core_own):
                for d in far_first:
                    planes(d, h, body)

    def last(h):
        for step in range(1, dps):
            dp_arrive(lax.rem(dp + step, dps), h)
        total = dp_in[0, spans[h]].astype(f32)
        for index in range(1, dps):
            total = total + dp_in[index, spans[h]].astype(f32)
        leave(h, spans[h], total)

    def steps(h):
        found = []
        for d in far_first:
            found.append(lambda d=d: planes(d, h, send_across))
            if d + 1 < height:
                found.append(lambda d=d: planes(d + 1, h, send_line))
        found.append(lambda: planes(0, h, send_line))
        found.append(lambda: last(h))
        return found

    def settle(z, h, way):
        core_copy(z, 0, h).wait_send()
        core_copy(z, 1, h).wait_send()
        across_copy(z, h).wait_send()
        if way is not None:
            line_copy(z, 0, h, place.up).wait_send()

    def finish():
        for h in range(HALVES):
            for d in far_first:
                planes(d, h, settle)
            for step in range(1, dps):
                dp_copy(step, h).wait_send()

    return begin, steps, finish


def scatter_scratch(n, rows, width):
    height = n // (CORES * COLUMNS)
    dps = lax.axis_size("dp")
    sizes = [height * COLUMNS, height, height, height, height + 1, dps]
    sems = [height * COLUMNS] * 2 + [height] * 3 + [height + 1] + [dps] * 2
    return (
        [pltpu.VMEM((size, rows, width), jnp.bfloat16) for size in sizes],
        [pltpu.SemaphoreType.DMA((size, HALVES)) for size in sems],
    )


def gather_scratch(n, pieces):
    return [pltpu.SemaphoreType.DMA((pieces, 4, n)), pltpu.SemaphoreType.DMA((pieces, n))]


def token_pieces(ref):
    rows = ref.shape[1] // HALVES
    return [lambda block, h=h: ref.at[block, pl.ds(h * rows, rows)] for h in range(HALVES)]


def load(sems, *pairs):
    copies = [
        pltpu.make_async_copy(source, target, sems.at[i])
        for i, (source, target) in enumerate(pairs)
    ]
    for copy in copies:
        copy.start()
    return copies


def table_matches(place, tables_ref, block, capacity):
    places = tables_ref[block, pl.ds(place.me, 1), :]
    spots = lax.broadcasted_iota(jnp.int32, (capacity, places.shape[1]), 0).astype(jnp.float32)
    return places == spots


def forward_kernel(
    n,
    capacity,
    tokens_ref,
    routes_ref,
    gates_ref,
    w_gate_in,
    w_up_in,
    w_down_in,
    tables_ref,
    slot_rows_out,
    gate_out,
    up_out,
    hidden_out,
    outs_out,
    rows_ref,
    slot_rows_ref,
    gate_ref,
    up_ref,
    hidden_ref,
    outs_ref,
    w_gate_ref,
    w_up_ref,
    w_down_ref,
    send,
    recv,
    leaving,
    loading,
):
    place = Place(n)
    group = CORES * COLUMNS
    bf16, f32 = jnp.bfloat16, jnp.float32
    loads = load(
        loading, (w_gate_in, w_gate_ref), (w_up_in, w_up_ref), (w_down_in, w_down_ref)
    )
    rows_ref[place.me] = tokens_ref[...]
    tables_ref[place.me] = table_of(routes_ref[...], gates_ref[...].astype(f32), n)
    greet(place)
    pieces = [lambda block: tables_ref.at[block]] + token_pieces(rows_ref)
    spread = Gather(place, pieces, send, recv)
    results = [
        (slot_rows_ref, slot_rows_out),
        (gate_ref, gate_out),
        (up_ref, up_out),
        (hidden_ref, hidden_out),
        (outs_ref, outs_out),
    ]

    def copies_out(z):
        return [
            pltpu.make_async_copy(source.at[z], target.at[z], leaving.at[i, z])
            for i, (source, target) in enumerate(results)
        ]

    def matches(block):
        return table_matches(place, tables_ref, block, capacity)

    def compute(z):
        spread.from_sibling(z)
        for i in range(group):
            block = z * group + i
            select = jnp.where(matches(block), 1.0, 0.0).astype(bf16)
            slot_rows_ref[z, pl.ds(i * capacity, capacity)] = jnp.dot(
                select, rows_ref[block], preferred_element_type=f32
            ).astype(bf16)
        gate_pre = jnp.dot(slot_rows_ref[z], w_gate_ref[0], preferred_element_type=f32)
        up_pre = jnp.dot(slot_rows_ref[z], w_up_ref[0], preferred_element_type=f32)
        gate_ref[z] = gate_pre
        up_ref[z] = up_pre
        hidden = (gate_pre * jax.nn.sigmoid(gate_pre) * up_pre).astype(bf16)
        hidden_ref[z] = hidden
        part = jnp.dot(hidden, w_down_ref[0], preferred_element_type=f32).astype(bf16)
        for i in range(group):
            block = z * group + i
            gates = tables_ref[block, pl.ds(place.me + n, 1), :]
            gated = jnp.where(matches(block), gates, 0.0).astype(bf16)
            outs_ref[z, i] = lax.dot_general(
                gated,
                part[i * capacity : (i + 1) * capacity],
                (((0,), (0,)), ((), ())),
                preferred_element_type=f32,
            ).astype(bf16)
        for copy in copies_out(z):
            copy.start()

    for piece in range(len(pieces)):
        spread.begin(piece)
    spread.run(compute, loads)
    for z in range(place.height):
        for copy in copies_out(z):
            copy.wait()


def middle_kernel(
    n,
    capacity,
    targets_ref,
    scales_ref,
    tables_ref,
    part_in,
    gate_in,
    up_in,
    w_gate_in,
    w_up_in,
    w_down_in,
    slot_grads_out,
    gate_grad_out,
    up_grad_out,
    backs_out,
    grads_ref,
    part_ref,
    gate_ref,
    up_ref,
    w_gate_ref,
    w_up_ref,
    w_down_ref,
    slot_grads_ref,
    gate_grad_ref,
    up_grad_ref,
    *scratch,
):
    place = Place(n)
    group = CORES * COLUMNS
    bf16, f32 = jnp.bfloat16, jnp.float32
    contract_last = (((1,), (1,)), ((), ()))
    bufs, sems, (send, recv, leaving, loading) = scratch[:6], scratch[6:14], scratch[14:]
    loads = load(
        loading,
        (part_in, part_ref),
        (gate_in, gate_ref),
        (up_in, up_ref),
        (w_gate_in, w_gate_ref),
        (w_up_in, w_up_ref),
        (w_down_in, w_down_ref),
    )
    greet(place)
    spread = Gather(place, token_pieces(grads_ref), send, recv)
    loads[0].wait()

    def leave(h, span, total):
        error = total - targets_ref[span, :].astype(f32)
        grads_ref[place.me, span] = (scales_ref[span, :] * error).astype(bf16)
        spread.begin(h)

    begin, steps, finish = scatter(place, part_ref, bufs, sems, leave)
    begin()
    staggered(steps(0), steps(1), 1)
    finish()

    def copies_out(z):
        blocks = pl.ds(z * group, group)
        pairs = [
            (slot_grads_ref.at[z], slot_grads_out.at[z]),
            (gate_grad_ref.at[z], gate_grad_out.at[z]),
            (up_grad_ref.at[z], up_grad_out.at[z]),
            (part_ref.at[blocks], backs_out.at[blocks]),
        ]
        return [
            pltpu.make_async_copy(source, target, leaving.at[i, z])
            for i, (source, target) in enumerate(pairs)
        ]

    def compute(z):
        spread.from_sibling(z)
        for i in range(group):
            block = z * group + i
            gates = tables_ref[block, pl.ds(place.me + n, 1), :]
            hits = table_matches(place, tables_ref, block, capacity)
            slot_grads_ref[z, pl.ds(i * capacity, capacity)] = jnp.dot(
                jnp.where(hits, gates, 0.0).astype(bf16), grads_ref[block], preferred_element_type=f32
            ).astype(bf16)
        hidden_grad = lax.dot_general(
            slot_grads_ref[z], w_down_ref[0], contract_last, preferred_element_type=f32
        )
        gate_pre = gate_ref[z]
        sigma = jax.nn.sigmoid(gate_pre)
        gate_grad = hidden_grad * up_ref[z] * sigma * (1.0 + gate_pre * (1.0 - sigma))
        gate_grad = gate_grad.astype(bf16)
        up_grad = (hidden_grad * gate_pre * sigma).astype(bf16)
        gate_grad_ref[z] = gate_grad
        up_grad_ref[z] = up_grad
        row_part = lax.dot_general(
            gate_grad, w_gate_ref[0], contract_last, preferred_element_type=f32
        )
        row_part = row_part + lax.dot_general(
            up_grad, w_up_ref[0], contract_last, preferred_element_type=f32
        )
        row_part = row_part.astype(bf16)
        for i in range(group):
            block = z * group + i
            hits = table_matches(place, tables_ref, block, capacity)
            part_ref[block] = lax.dot_general(
                jnp.where(hits, 1.0, 0.0).astype(bf16),
                row_part[i * capacity : (i + 1) * capacity],
                (((0,), (0,)), ((), ())),
                preferred_element_type=f32,
            ).astype(bf16)
        for copy in copies_out(z):
            copy.start()

    spread.run(compute, loads[1:])
    for z in range(place.height):
        for copy in copies_out(z):
            copy.wait()


def loss_kernel(n, part_ref, targets_ref, scales_ref, grads_ref, *scratch):
    place = Place(n)
    bufs, sems, (send, recv) = scratch[:6], scratch[6:14], scratch[14:]
    greet(place)
    spread = Gather(place, token_pieces(grads_ref), send, recv)

    def leave(h, span, total):
        error = total - targets_ref[span, :].astype(jnp.float32)
        grads_ref[place.me, span] = (scales_ref[span, :] * error).astype(jnp.bfloat16)
        spread.begin(h)

    begin, steps, finish = scatter(place, part_ref, bufs, sems, leave)
    begin()
    staggered(steps(0) + spread.steps(0), steps(1) + spread.steps(1), 4)
    for z in range(place.height):
        spread.from_sibling(z)
    spread.settle()
    finish()


def return_kernel(n, part_ref, out_ref, *scratch):
    place = Place(n)
    bufs, sems = scratch[:6], scratch[6:14]
    greet(place)

    def leave(h, span, total):
        out_ref[span, :] = total.astype(jnp.bfloat16)

    begin, steps, finish = scatter(place, part_ref, bufs, sems, leave)
    begin()
    staggered(steps(0), steps(1), 1)
    finish()


def run(kernel, out_shape, scratch, number, *operands, in_vmem=None, out_vmem=None):
    whole = pl.BlockSpec(memory_space=pltpu.VMEM)
    outside = pl.BlockSpec(memory_space=pl.ANY)

    def places(count, near):
        near = count if near is None else near
        return [whole] * near + [outside] * (count - near)

    return pl.pallas_call(
        kernel,
        out_shape=out_shape,
        in_specs=places(len(operands), in_vmem),
        out_specs=places(len(out_shape), out_vmem),
        scratch_shapes=scratch,
        compiler_params=pltpu.CompilerParams(
            collective_id=number, has_side_effects=True, vmem_limit_bytes=60 * 2**20
        ),
    )(*operands)


def table_of(routes, gates, experts):
    top, count = routes.shape
    ids = lax.broadcasted_iota(jnp.int32, (experts, count), 0)
    chosen = jnp.zeros((experts, count), jnp.float32)
    weights = jnp.zeros((experts, count), jnp.float32)
    for k in range(top):
        hit = routes[k : k + 1, :] == ids
        chosen = jnp.where(hit, 1.0, chosen)
        weights = jnp.where(hit, gates[k : k + 1, :], weights)
    square = (count, count)
    earlier = lax.broadcasted_iota(jnp.int32, square, 0) < lax.broadcasted_iota(jnp.int32, square, 1)
    places = jnp.dot(
        chosen.astype(jnp.bfloat16),
        jnp.where(earlier, 1.0, 0.0).astype(jnp.bfloat16),
        preferred_element_type=jnp.float32,
    )
    return jnp.concatenate([jnp.where(chosen > 0.0, places, -1.0), weights], 0)


def block_dot(left, right, contract):
    return lax.dot_general(
        left, right, ((contract[0], contract[1]), ((0,), (0,))), preferred_element_type=jnp.float32
    ).astype(jnp.bfloat16)


def shards(tokens, routes, route_gates, domains, domain_weight, targets, w_gate, w_up, w_down):
    count, width = tokens.shape
    n = lax.axis_size("expert")
    capacity = max(2, 4 * count * routes.shape[1] // (3 * n))
    bf16, f32 = jnp.bfloat16, jnp.float32
    weights = (w_gate, w_up, w_down)
    contract_last = (((1,), (1,)), ((), ()))
    contract_first = (((0,), (0,)), ((), ()))

    height = n // (CORES * COLUMNS)
    slots = n * capacity // height
    hidden_width = w_gate.shape[2]
    shapes = [
        ((height, slots, width), bf16),
        ((height, slots, hidden_width), f32),
        ((height, slots, hidden_width), f32),
        ((height, slots, hidden_width), bf16),
        ((height, n // height, count, width), bf16),
    ]
    tables, slot_rows, gate_pre, up_pre, hidden, outs = run(
        functools.partial(forward_kernel, n, capacity),
        [jax.ShapeDtypeStruct((n, 2 * n, count), f32)]
        + [jax.ShapeDtypeStruct(*shape) for shape in shapes],
        [pltpu.VMEM((n, count, width), bf16)]
        + [pltpu.VMEM(*shape) for shape in shapes]
        + [pltpu.VMEM(item.shape, bf16) for item in weights]
        + gather_scratch(n, HALVES + 1)
        + [pltpu.SemaphoreType.DMA((len(shapes), height)), pltpu.SemaphoreType.DMA((3,))],
        0,
        tokens,
        routes.T,
        route_gates.T,
        *weights,
        in_vmem=3,
        out_vmem=1,
    )
    outs = outs.reshape(n, count, width)
    picks = domains[:, None] == jnp.arange(domain_weight.shape[0], dtype=jnp.int32)[None, :]
    scales = jnp.sum(jnp.where(picks, domain_weight[None, :], 0.0), 1, keepdims=True)
    bufs, sems = scatter_scratch(n, count, width)
    grad_shapes = [
        ((height, slots, width), bf16),
        ((height, slots, hidden_width), bf16),
        ((height, slots, hidden_width), bf16),
    ]
    needed = (
        [((n, count, width), bf16)] * 2
        + [((height, slots, hidden_width), f32)] * 2
        + [(item.shape, bf16) for item in weights]
        + grad_shapes
    )
    fits = sum(math.prod(shape) * (4 if kind == f32 else 2) for shape, kind in needed)
    fits = fits + sum(math.prod(buf.shape) * 2 for buf in bufs) < 48 * 2**20
    if fits:
        slot_grads, gate_grad, up_grad, backs = run(
            functools.partial(middle_kernel, n, capacity),
            [jax.ShapeDtypeStruct(*shape) for shape in grad_shapes + needed[:1]],
            [pltpu.VMEM(*shape) for shape in needed]
            + bufs
            + sems
            + gather_scratch(n, HALVES)
            + [pltpu.SemaphoreType.DMA((4, height)), pltpu.SemaphoreType.DMA((6,))],
            1,
            targets,
            scales,
            tables,
            outs,
            gate_pre,
            up_pre,
            *weights,
            in_vmem=3,
            out_vmem=0,
        )
        slot_grads = slot_grads.reshape(n * capacity, width)
        gate_grad = gate_grad.reshape(n * capacity, hidden_width)
        up_grad = up_grad.reshape(n * capacity, hidden_width)
    slot_rows = slot_rows.reshape(n * capacity, width)
    gate_pre, up_pre, hidden = (
        item.reshape(n * capacity, hidden_width) for item in (gate_pre, up_pre, hidden)
    )
    if not fits:
        me = lax.axis_index("expert")
        places = lax.dynamic_index_in_dim(tables, me, 1, keepdims=True)
        gates = lax.dynamic_index_in_dim(tables, me + n, 1, keepdims=True)
        matches = places == jnp.arange(capacity, dtype=f32)[None, :, None]
        select = matches.astype(bf16)
        gated = jnp.where(matches, gates, 0.0).astype(bf16)

        (loss_grads,) = run(
            functools.partial(loss_kernel, n),
            [jax.ShapeDtypeStruct((n, count, width), bf16)],
            bufs + sems + gather_scratch(n, HALVES),
            1,
            outs,
            targets,
            scales,
        )

        slot_grads = block_dot(gated, loss_grads, ((2,), (1,))).reshape(n * capacity, width)
        hidden_grad = lax.dot_general(slot_grads, w_down[0], contract_last, preferred_element_type=f32)
        sigma = jax.nn.sigmoid(gate_pre)
        gate_grad = (hidden_grad * up_pre * sigma * (1.0 + gate_pre * (1.0 - sigma))).astype(bf16)
        up_grad = (hidden_grad * gate_pre * sigma).astype(bf16)
        row_part = lax.dot_general(gate_grad, w_gate[0], contract_last, preferred_element_type=f32)
        row_part = row_part + lax.dot_general(up_grad, w_up[0], contract_last, preferred_element_type=f32)
        backs = block_dot(select, row_part.astype(bf16).reshape(n, capacity, width), ((1,), (1,)))
    (grad_tokens,) = run(
        functools.partial(return_kernel, n),
        [jax.ShapeDtypeStruct((count, width), bf16)],
        bufs + sems,
        2,
        backs,
    )
    grad_down = lax.dot_general(hidden, slot_grads, contract_first, preferred_element_type=f32)
    grad_gate = lax.dot_general(slot_rows, gate_grad, contract_first, preferred_element_type=f32)
    grad_up = lax.dot_general(slot_rows, up_grad, contract_first, preferred_element_type=f32)
    return grad_tokens, grad_gate[None], grad_up[None], grad_down[None]


def solution(mesh):
    return jax.shard_map(
        shards,
        mesh=mesh,
        in_specs=(
            P("expert", None),
            P("expert", None),
            P("expert", None),
            P("expert"),
            P(),
            P("expert", None),
            P("expert", None, "dp"),
            P("expert", None, "dp"),
            P("expert", "dp", None),
        ),
        out_specs=(
            P("expert", None),
            P("expert", None, "dp"),
            P("expert", None, "dp"),
            P("expert", "dp", None),
        ),
        check_vma=False,
    )
```

```python
import functools
import math

import jax
import jax.numpy as jnp
from jax import lax
from jax.experimental import pallas as pl
from jax.experimental.pallas import tpu as pltpu
from jax.sharding import PartitionSpec as P

MESH = pl.DeviceIdType.MESH
CORES = 2
COLUMNS = 2
HALVES = 2
UP, DOWN, ACROSS, SIBLING = range(4)


class Place:
    def __init__(self, n):
        self.n = n
        self.height = n // (CORES * COLUMNS)
        self.me = lax.axis_index("expert")
        self.core = lax.rem(self.me, CORES)
        self.x = lax.rem(self.me // CORES, COLUMNS)
        self.z = self.me // (CORES * COLUMNS)
        self.up = self.me + CORES * COLUMNS
        self.down = self.me - CORES * COLUMNS
        self.has_up = self.z + 1 < self.height
        self.has_down = self.z > 0
        self.across = self.at(self.z, 1 - self.x, self.core)
        self.sibling = self.at(self.z, self.x, 1 - self.core)

    def at(self, z, x, core):
        return (z * COLUMNS + x) * CORES + core

    def by_distance(self, d):
        if d == 0:
            return [(self.z, None)]
        return [(self.z - d, self.z - d >= 0), (self.z + d, self.z + d < self.height)]


def when(condition, body):
    if condition is None:
        body()
    else:
        pl.when(condition)(body)


def greet(place):
    barrier = pltpu.get_barrier_semaphore()

    def signal(target):
        pl.semaphore_signal(barrier, inc=1, device_id=target, device_id_type=MESH)

    pl.when(place.has_up)(lambda: signal({"expert": place.up}))
    pl.when(place.has_down)(lambda: signal({"expert": place.down}))
    signal({"expert": place.across})
    signal({"expert": place.sibling})
    count = 2 + place.has_up.astype(jnp.int32) + place.has_down.astype(jnp.int32)
    dps = lax.axis_size("dp")
    for step in range(1, dps):
        signal({"dp": lax.rem(lax.axis_index("dp") + step, dps)})
    count = count + (dps - 1)
    pl.semaphore_wait(barrier, count)


class Gather:
    def __init__(self, place, pieces, send, recv):
        self.place, self.pieces, self.send, self.recv = place, pieces, send, recv

    def copy(self, piece, block, link):
        place = self.place
        view = self.pieces[piece](block)
        target = (place.up, place.down, place.across, place.sibling)[link]
        return pltpu.make_async_remote_copy(
            src_ref=view,
            dst_ref=view,
            send_sem=self.send.at[piece, link, block],
            recv_sem=self.recv.at[piece, block],
            device_id={"expert": target},
            device_id_type=MESH,
        )

    def arrive(self, piece, block):
        self.copy(piece, block, SIBLING).wait_recv()

    def mine(self, z):
        return self.place.at(z, self.place.x, self.place.core)

    def other(self, z):
        return self.place.at(z, 1 - self.place.x, self.place.core)

    def begin(self, piece):
        place, me = self.place, self.place.me
        pl.when(place.has_up)(lambda: self.copy(piece, me, UP).start())
        pl.when(place.has_down)(lambda: self.copy(piece, me, DOWN).start())
        self.copy(piece, me, ACROSS).start()
        self.copy(piece, me, SIBLING).start()

    def line_step(self, d, piece):
        place = self.place
        for (z, there), onward, open_ in zip(
            place.by_distance(d), (UP, DOWN), (place.has_up, place.has_down)
        ):

            def body(z=z, onward=onward, open_=open_):
                self.arrive(piece, self.mine(z))
                pl.when(open_)(lambda: self.copy(piece, self.mine(z), onward).start())
                self.copy(piece, self.mine(z), ACROSS).start()
                self.copy(piece, self.mine(z), SIBLING).start()

            when(there, body)

    def across_step(self, d, piece):
        for z, there in self.place.by_distance(d):

            def body(z=z):
                self.arrive(piece, self.other(z))
                self.copy(piece, self.other(z), SIBLING).start()

            when(there, body)

    def from_sibling(self, z):
        for piece in range(len(self.pieces)):
            for x in range(COLUMNS):
                self.arrive(piece, self.place.at(z, x, 1 - self.place.core))

    def steps(self, piece):
        height = self.place.height
        found = []
        for d in range(1, height):
            found.append(lambda d=d: self.line_step(d, piece))
            found.append(lambda d=d: self.across_step(d - 1, piece))
        found.append(lambda: self.across_step(height - 1, piece))
        return found

    def run(self, compute, loads):
        place = self.place
        for d in range(1, place.height + 1):
            for piece in range(len(self.pieces)):
                if d < place.height:
                    self.line_step(d, piece)
                self.across_step(d - 1, piece)
            if d == 1:
                for copy in loads:
                    copy.wait()
                compute(place.z)
                continue

            @pl.loop(0, 2)
            def _(side, d=d):
                z = place.z + (2 * side - 1) * (d - 1)
                pl.when(jnp.logical_and(z >= 0, z < place.height))(lambda: compute(z))

        self.settle()

    def settle(self):
        place = self.place
        for z in range(place.height):
            for piece in range(len(self.pieces)):
                self.copy(piece, self.mine(z), ACROSS).wait_send()
                self.copy(piece, self.mine(z), SIBLING).wait_send()
                self.copy(piece, self.other(z), SIBLING).wait_send()
                pl.when(jnp.logical_and(place.has_up, z <= place.z))(
                    lambda: self.copy(piece, self.mine(z), UP).wait_send()
                )
                pl.when(jnp.logical_and(place.has_down, z >= place.z))(
                    lambda: self.copy(piece, self.mine(z), DOWN).wait_send()
                )


def staggered(first, second, lag):
    for i in range(max(len(first), len(second) + lag)):
        if i < len(first):
            first[i]()
        if i >= lag and i - lag < len(second):
            second[i - lag]()


def scatter(place, part_ref, bufs, sems, leave):
    core_in, across_out, across_in, line_out, line_in, dp_in = bufs
    core_send, core_recv, across_send, across_recv, line_send, line_recv, dp_send, dp_recv = sems
    height = place.height
    rows = part_ref.shape[1] // HALVES
    dps = lax.axis_size("dp")
    dp = lax.axis_index("dp")
    spans = [pl.ds(h * rows, rows) for h in range(HALVES)]
    f32 = jnp.float32

    def core_copy(z, x, h):
        spot = z * COLUMNS + x
        return pltpu.make_async_remote_copy(
            src_ref=part_ref.at[place.at(z, x, 1 - place.core), spans[h]],
            dst_ref=core_in.at[spot, spans[h]],
            send_sem=core_send.at[spot, h],
            recv_sem=core_recv.at[spot, h],
            device_id={"expert": place.sibling},
            device_id_type=MESH,
        )

    def across_copy(z, h):
        return pltpu.make_async_remote_copy(
            src_ref=across_out.at[z, spans[h]],
            dst_ref=across_in.at[z, spans[h]],
            send_sem=across_send.at[z, h],
            recv_sem=across_recv.at[z, h],
            device_id={"expert": place.across},
            device_id_type=MESH,
        )

    def line_copy(z, slot, h, target):
        return pltpu.make_async_remote_copy(
            src_ref=line_out.at[z, spans[h]],
            dst_ref=line_in.at[slot, spans[h]],
            send_sem=line_send.at[z, h],
            recv_sem=line_recv.at[slot, h],
            device_id={"expert": target},
            device_id_type=MESH,
        )

    def line_arrive(slot, h):
        line_copy(0, slot, h, place.up).wait_recv()

    def dp_copy(step, h):
        return pltpu.make_async_remote_copy(
            src_ref=dp_in.at[dp, spans[h]],
            dst_ref=dp_in.at[dp, spans[h]],
            send_sem=dp_send.at[step, h],
            recv_sem=dp_recv.at[dp, h],
            device_id={"dp": lax.rem(dp + step, dps)},
            device_id_type=MESH,
        )

    def dp_arrive(index, h):
        pltpu.make_async_remote_copy(
            src_ref=dp_in.at[dp, spans[h]],
            dst_ref=dp_in.at[index, spans[h]],
            send_sem=dp_send.at[1, h],
            recv_sem=dp_recv.at[index, h],
            device_id={"dp": lax.rem(dp + 1, dps)},
            device_id_type=MESH,
        ).wait_recv()

    def planes(d, h, body):
        for way, (z, there) in enumerate(place.by_distance(d)):
            when(there, lambda z=z: body(z, h, None if d == 0 else (DOWN, UP)[way]))

    def send_core(z, h, way):
        core_copy(z, 1 - place.x, h).start()

    def send_core_own(z, h, way):
        core_copy(z, place.x, h).start()

    def send_across(z, h, way):
        core_copy(z, 1 - place.x, h).wait_recv()
        span = spans[h]
        total = part_ref[place.at(z, 1 - place.x, place.core), span].astype(f32)
        total = total + core_in[z * COLUMNS + 1 - place.x, span].astype(f32)
        across_out[z, span] = total.astype(jnp.bfloat16)
        across_copy(z, h).start()

    def send_line(z, h, way):
        span = spans[h]
        core_copy(z, place.x, h).wait_recv()
        across_copy(z, h).wait_recv()

        def total():
            own = part_ref[place.at(z, place.x, place.core), span].astype(f32)
            own = own + core_in[z * COLUMNS + place.x, span].astype(f32)
            return own + across_in[z, span].astype(f32)

        if way is None:

            def store(value):
                dp_in[dp, span] = value.astype(jnp.bfloat16)

            def both():
                line_arrive(z, h)
                line_arrive(height, h)
                store(total() + line_in[z, span].astype(f32) + line_in[height, span].astype(f32))

            def above():
                line_arrive(z, h)
                store(total() + line_in[z, span].astype(f32))

            def below():
                line_arrive(height, h)
                store(total() + line_in[height, span].astype(f32))

            pl.when(jnp.logical_and(place.has_up, place.has_down))(both)
            pl.when(jnp.logical_and(place.has_up, jnp.logical_not(place.has_down)))(above)
            pl.when(jnp.logical_and(jnp.logical_not(place.has_up), place.has_down))(below)
            for step in range(1, dps):
                dp_copy(step, h).start()
            return
        if way == DOWN:
            before, slot, target = place.has_up, z, place.down
        else:
            before, target = place.has_down, place.up
            slot = jnp.where(z == place.z + 1, height, z)

        def with_arrival():
            line_arrive(z, h)
            line_out[z, span] = (total() + line_in[z, span].astype(f32)).astype(jnp.bfloat16)

        def alone():
            line_out[z, span] = total().astype(jnp.bfloat16)

        pl.when(before)(with_arrival)
        pl.when(jnp.logical_not(before))(alone)
        line_copy(z, slot, h, target).start()

    far_first = list(range(height - 1, -1, -1))

    def begin():
        for h in range(HALVES):
            for body in (send_core, send_core_own):
                for d in far_first:
                    planes(d, h, body)

    def last(h):
        for step in range(1, dps):
            dp_arrive(lax.rem(dp + step, dps), h)
        total = dp_in[0, spans[h]].astype(f32)
        for index in range(1, dps):
            total = total + dp_in[index, spans[h]].astype(f32)
        leave(h, spans[h], total)

    def steps(h):
        found = []
        for d in far_first:
            found.append(lambda d=d: planes(d, h, send_across))
            if d + 1 < height:
                found.append(lambda d=d: planes(d + 1, h, send_line))
        found.append(lambda: planes(0, h, send_line))
        found.append(lambda: last(h))
        return found

    def settle(z, h, way):
        core_copy(z, 0, h).wait_send()
        core_copy(z, 1, h).wait_send()
        across_copy(z, h).wait_send()
        if way is not None:
            line_copy(z, 0, h, place.up).wait_send()

    def finish():
        for h in range(HALVES):
            for d in far_first:
                planes(d, h, settle)
            for step in range(1, dps):
                dp_copy(step, h).wait_send()

    return begin, steps, finish


def scatter_scratch(n, rows, width):
    height = n // (CORES * COLUMNS)
    dps = lax.axis_size("dp")
    sizes = [height * COLUMNS, height, height, height, height + 1, dps]
    sems = [height * COLUMNS] * 2 + [height] * 3 + [height + 1] + [dps] * 2
    return (
        [pltpu.VMEM((size, rows, width), jnp.bfloat16) for size in sizes],
        [pltpu.SemaphoreType.DMA((size, HALVES)) for size in sems],
    )


def gather_scratch(n, pieces):
    return [pltpu.SemaphoreType.DMA((pieces, 4, n)), pltpu.SemaphoreType.DMA((pieces, n))]


def token_pieces(ref):
    rows = ref.shape[1] // HALVES
    return [lambda block, h=h: ref.at[block, pl.ds(h * rows, rows)] for h in range(HALVES)]


def upright(row):
    square = (row.shape[1], row.shape[1])
    diagonal = lax.broadcasted_iota(jnp.int32, square, 0) == lax.broadcasted_iota(jnp.int32, square, 1)
    return jnp.sum(jnp.where(diagonal, row, 0.0), 1, keepdims=True)


def token_scales(domains, domain_weight):
    shape = (domain_weight.shape[1], domains.shape[1])
    picks = lax.broadcasted_iota(jnp.int32, shape, 0) == domains
    return upright(jnp.sum(jnp.where(picks, upright(domain_weight), 0.0), 0, keepdims=True))


def load(sems, *pairs):
    copies = [
        pltpu.make_async_copy(source, target, sems.at[i])
        for i, (source, target) in enumerate(pairs)
    ]
    for copy in copies:
        copy.start()
    return copies


def table_matches(place, tables_ref, block, capacity):
    places = tables_ref[block, pl.ds(place.me, 1), :]
    spots = lax.broadcasted_iota(jnp.int32, (capacity, places.shape[1]), 0).astype(jnp.float32)
    return places == spots


def forward_kernel(
    n,
    capacity,
    tokens_ref,
    routes_ref,
    gates_ref,
    w_gate_in,
    w_up_in,
    w_down_in,
    tables_ref,
    slot_rows_out,
    gate_out,
    up_out,
    hidden_out,
    outs_out,
    rows_ref,
    slot_rows_ref,
    gate_ref,
    up_ref,
    hidden_ref,
    outs_ref,
    w_gate_ref,
    w_up_ref,
    w_down_ref,
    send,
    recv,
    leaving,
    loading,
):
    place = Place(n)
    group = CORES * COLUMNS
    bf16, f32 = jnp.bfloat16, jnp.float32
    loads = load(
        loading, (w_gate_in, w_gate_ref), (w_up_in, w_up_ref), (w_down_in, w_down_ref)
    )
    rows_ref[place.me] = tokens_ref[...]
    tables_ref[place.me] = table_of(routes_ref[...], gates_ref[...].astype(f32), n)
    greet(place)
    pieces = [lambda block: tables_ref.at[block]] + token_pieces(rows_ref)
    spread = Gather(place, pieces, send, recv)
    results = [
        (slot_rows_ref, slot_rows_out),
        (gate_ref, gate_out),
        (up_ref, up_out),
        (hidden_ref, hidden_out),
        (outs_ref, outs_out),
    ]

    def copies_out(z):
        return [
            pltpu.make_async_copy(source.at[z], target.at[z], leaving.at[i, z])
            for i, (source, target) in enumerate(results)
        ]

    def matches(block):
        return table_matches(place, tables_ref, block, capacity)

    def compute(z):
        spread.from_sibling(z)
        for i in range(group):
            block = z * group + i
            select = jnp.where(matches(block), 1.0, 0.0).astype(bf16)
            slot_rows_ref[z, pl.ds(i * capacity, capacity)] = jnp.dot(
                select, rows_ref[block], preferred_element_type=f32
            ).astype(bf16)
        gate_pre = jnp.dot(slot_rows_ref[z], w_gate_ref[0], preferred_element_type=f32)
        up_pre = jnp.dot(slot_rows_ref[z], w_up_ref[0], preferred_element_type=f32)
        gate_ref[z] = gate_pre
        up_ref[z] = up_pre
        hidden = (gate_pre * jax.nn.sigmoid(gate_pre) * up_pre).astype(bf16)
        hidden_ref[z] = hidden
        part = jnp.dot(hidden, w_down_ref[0], preferred_element_type=f32).astype(bf16)
        for i in range(group):
            block = z * group + i
            gates = tables_ref[block, pl.ds(place.me + n, 1), :]
            gated = jnp.where(matches(block), gates, 0.0).astype(bf16)
            outs_ref[z, i] = lax.dot_general(
                gated,
                part[i * capacity : (i + 1) * capacity],
                (((0,), (0,)), ((), ())),
                preferred_element_type=f32,
            ).astype(bf16)
        for copy in copies_out(z):
            copy.start()

    for piece in range(len(pieces)):
        spread.begin(piece)
    spread.run(compute, loads)
    for z in range(place.height):
        for copy in copies_out(z):
            copy.wait()


def middle_kernel(
    n,
    capacity,
    targets_ref,
    domains_ref,
    domain_weight_ref,
    tables_ref,
    part_in,
    gate_in,
    up_in,
    w_gate_in,
    w_up_in,
    w_down_in,
    slot_grads_out,
    gate_grad_out,
    up_grad_out,
    backs_out,
    grads_ref,
    part_ref,
    gate_ref,
    up_ref,
    w_gate_ref,
    w_up_ref,
    w_down_ref,
    slot_grads_ref,
    gate_grad_ref,
    up_grad_ref,
    *scratch,
):
    place = Place(n)
    group = CORES * COLUMNS
    bf16, f32 = jnp.bfloat16, jnp.float32
    contract_last = (((1,), (1,)), ((), ()))
    bufs, sems, (send, recv, leaving, loading) = scratch[:6], scratch[6:14], scratch[14:]
    loads = load(
        loading,
        (part_in, part_ref),
        (gate_in, gate_ref),
        (up_in, up_ref),
        (w_gate_in, w_gate_ref),
        (w_up_in, w_up_ref),
        (w_down_in, w_down_ref),
    )
    greet(place)
    spread = Gather(place, token_pieces(grads_ref), send, recv)
    loads[0].wait()

    scales = token_scales(domains_ref[...], domain_weight_ref[...])
    rows = targets_ref.shape[0] // HALVES

    def leave(h, span, total):
        error = total - targets_ref[span, :].astype(f32)
        grads_ref[place.me, span] = (scales[h * rows : (h + 1) * rows] * error).astype(bf16)
        spread.begin(h)

    begin, steps, finish = scatter(place, part_ref, bufs, sems, leave)
    begin()
    staggered(steps(0), steps(1), 1)
    finish()

    def copies_out(z):
        blocks = pl.ds(z * group, group)
        pairs = [
            (slot_grads_ref.at[z], slot_grads_out.at[z]),
            (gate_grad_ref.at[z], gate_grad_out.at[z]),
            (up_grad_ref.at[z], up_grad_out.at[z]),
            (part_ref.at[blocks], backs_out.at[blocks]),
        ]
        return [
            pltpu.make_async_copy(source, target, leaving.at[i, z])
            for i, (source, target) in enumerate(pairs)
        ]

    def compute(z):
        spread.from_sibling(z)
        for i in range(group):
            block = z * group + i
            gates = tables_ref[block, pl.ds(place.me + n, 1), :]
            hits = table_matches(place, tables_ref, block, capacity)
            slot_grads_ref[z, pl.ds(i * capacity, capacity)] = jnp.dot(
                jnp.where(hits, gates, 0.0).astype(bf16), grads_ref[block], preferred_element_type=f32
            ).astype(bf16)
        hidden_grad = lax.dot_general(
            slot_grads_ref[z], w_down_ref[0], contract_last, preferred_element_type=f32
        )
        gate_pre = gate_ref[z]
        sigma = jax.nn.sigmoid(gate_pre)
        gate_grad = hidden_grad * up_ref[z] * sigma * (1.0 + gate_pre * (1.0 - sigma))
        gate_grad = gate_grad.astype(bf16)
        up_grad = (hidden_grad * gate_pre * sigma).astype(bf16)
        gate_grad_ref[z] = gate_grad
        up_grad_ref[z] = up_grad
        row_part = lax.dot_general(
            gate_grad, w_gate_ref[0], contract_last, preferred_element_type=f32
        )
        row_part = row_part + lax.dot_general(
            up_grad, w_up_ref[0], contract_last, preferred_element_type=f32
        )
        row_part = row_part.astype(bf16)
        for i in range(group):
            block = z * group + i
            hits = table_matches(place, tables_ref, block, capacity)
            part_ref[block] = lax.dot_general(
                jnp.where(hits, 1.0, 0.0).astype(bf16),
                row_part[i * capacity : (i + 1) * capacity],
                (((0,), (0,)), ((), ())),
                preferred_element_type=f32,
            ).astype(bf16)
        for copy in copies_out(z):
            copy.start()

    spread.run(compute, loads[1:])
    for z in range(place.height):
        for copy in copies_out(z):
            copy.wait()


def loss_kernel(
    n, part_ref, targets_ref, domains_ref, domain_weight_ref, grads_ref, *scratch
):
    place = Place(n)
    bufs, sems, (send, recv) = scratch[:6], scratch[6:14], scratch[14:]
    greet(place)
    spread = Gather(place, token_pieces(grads_ref), send, recv)

    scales = token_scales(domains_ref[...], domain_weight_ref[...])
    rows = targets_ref.shape[0] // HALVES

    def leave(h, span, total):
        error = total - targets_ref[span, :].astype(jnp.float32)
        grads_ref[place.me, span] = (scales[h * rows : (h + 1) * rows] * error).astype(jnp.bfloat16)
        spread.begin(h)

    begin, steps, finish = scatter(place, part_ref, bufs, sems, leave)
    begin()
    staggered(steps(0) + spread.steps(0), steps(1) + spread.steps(1), 4)
    for z in range(place.height):
        spread.from_sibling(z)
    spread.settle()
    finish()


def return_kernel(n, part_ref, out_ref, *scratch):
    place = Place(n)
    bufs, sems = scratch[:6], scratch[6:14]
    greet(place)

    def leave(h, span, total):
        out_ref[span, :] = total.astype(jnp.bfloat16)

    begin, steps, finish = scatter(place, part_ref, bufs, sems, leave)
    begin()
    staggered(steps(0), steps(1), 1)
    finish()


def run(kernel, out_shape, scratch, number, *operands, in_vmem=None, out_vmem=None):
    whole = pl.BlockSpec(memory_space=pltpu.VMEM)
    outside = pl.BlockSpec(memory_space=pl.ANY)

    def places(count, near):
        near = count if near is None else near
        return [whole] * near + [outside] * (count - near)

    return pl.pallas_call(
        kernel,
        out_shape=out_shape,
        in_specs=places(len(operands), in_vmem),
        out_specs=places(len(out_shape), out_vmem),
        scratch_shapes=scratch,
        compiler_params=pltpu.CompilerParams(
            collective_id=number, has_side_effects=True, vmem_limit_bytes=60 * 2**20
        ),
    )(*operands)


def table_of(routes, gates, experts):
    top, count = routes.shape
    ids = lax.broadcasted_iota(jnp.int32, (experts, count), 0)
    chosen = jnp.zeros((experts, count), jnp.float32)
    weights = jnp.zeros((experts, count), jnp.float32)
    for k in range(top):
        hit = routes[k : k + 1, :] == ids
        chosen = jnp.where(hit, 1.0, chosen)
        weights = jnp.where(hit, gates[k : k + 1, :], weights)
    square = (count, count)
    earlier = lax.broadcasted_iota(jnp.int32, square, 0) < lax.broadcasted_iota(jnp.int32, square, 1)
    places = jnp.dot(
        chosen.astype(jnp.bfloat16),
        jnp.where(earlier, 1.0, 0.0).astype(jnp.bfloat16),
        preferred_element_type=jnp.float32,
    )
    return jnp.concatenate([jnp.where(chosen > 0.0, places, -1.0), weights], 0)


def block_dot(left, right, contract):
    return lax.dot_general(
        left, right, ((contract[0], contract[1]), ((0,), (0,))), preferred_element_type=jnp.float32
    ).astype(jnp.bfloat16)


def shards(tokens, routes, route_gates, domains, domain_weight, targets, w_gate, w_up, w_down):
    count, width = tokens.shape
    n = lax.axis_size("expert")
    capacity = max(2, 4 * count * routes.shape[1] // (3 * n))
    bf16, f32 = jnp.bfloat16, jnp.float32
    weights = (w_gate, w_up, w_down)
    contract_last = (((1,), (1,)), ((), ()))
    contract_first = (((0,), (0,)), ((), ()))

    height = n // (CORES * COLUMNS)
    slots = n * capacity // height
    hidden_width = w_gate.shape[2]
    shapes = [
        ((height, slots, width), bf16),
        ((height, slots, hidden_width), f32),
        ((height, slots, hidden_width), f32),
        ((height, slots, hidden_width), bf16),
        ((height, n // height, count, width), bf16),
    ]
    tables, slot_rows, gate_pre, up_pre, hidden, outs = run(
        functools.partial(forward_kernel, n, capacity),
        [jax.ShapeDtypeStruct((n, 2 * n, count), f32)]
        + [jax.ShapeDtypeStruct(*shape) for shape in shapes],
        [pltpu.VMEM((n, count, width), bf16)]
        + [pltpu.VMEM(*shape) for shape in shapes]
        + [pltpu.VMEM(item.shape, bf16) for item in weights]
        + gather_scratch(n, HALVES + 1)
        + [pltpu.SemaphoreType.DMA((len(shapes), height)), pltpu.SemaphoreType.DMA((3,))],
        0,
        tokens,
        routes.T,
        route_gates.T,
        *weights,
        in_vmem=3,
        out_vmem=1,
    )
    outs = outs.reshape(n, count, width)
    loss_weights = (domains.reshape(1, -1), domain_weight.reshape(1, -1))
    bufs, sems = scatter_scratch(n, count, width)
    grad_shapes = [
        ((height, slots, width), bf16),
        ((height, slots, hidden_width), bf16),
        ((height, slots, hidden_width), bf16),
    ]
    needed = (
        [((n, count, width), bf16)] * 2
        + [((height, slots, hidden_width), f32)] * 2
        + [(item.shape, bf16) for item in weights]
        + grad_shapes
    )
    fits = sum(math.prod(shape) * (4 if kind == f32 else 2) for shape, kind in needed)
    fits = fits + sum(math.prod(buf.shape) * 2 for buf in bufs) < 48 * 2**20
    if fits:
        slot_grads, gate_grad, up_grad, backs = run(
            functools.partial(middle_kernel, n, capacity),
            [jax.ShapeDtypeStruct(*shape) for shape in grad_shapes + needed[:1]],
            [pltpu.VMEM(*shape) for shape in needed]
            + bufs
            + sems
            + gather_scratch(n, HALVES)
            + [pltpu.SemaphoreType.DMA((4, height)), pltpu.SemaphoreType.DMA((6,))],
            1,
            targets,
            *loss_weights,
            tables,
            outs,
            gate_pre,
            up_pre,
            *weights,
            in_vmem=4,
            out_vmem=0,
        )
        slot_grads = slot_grads.reshape(n * capacity, width)
        gate_grad = gate_grad.reshape(n * capacity, hidden_width)
        up_grad = up_grad.reshape(n * capacity, hidden_width)
    slot_rows = slot_rows.reshape(n * capacity, width)
    gate_pre, up_pre, hidden = (
        item.reshape(n * capacity, hidden_width) for item in (gate_pre, up_pre, hidden)
    )
    if not fits:
        me = lax.axis_index("expert")
        places = lax.dynamic_index_in_dim(tables, me, 1, keepdims=True)
        gates = lax.dynamic_index_in_dim(tables, me + n, 1, keepdims=True)
        matches = places == jnp.arange(capacity, dtype=f32)[None, :, None]
        select = matches.astype(bf16)
        gated = jnp.where(matches, gates, 0.0).astype(bf16)

        (loss_grads,) = run(
            functools.partial(loss_kernel, n),
            [jax.ShapeDtypeStruct((n, count, width), bf16)],
            bufs + sems + gather_scratch(n, HALVES),
            1,
            outs,
            targets,
            *loss_weights,
        )

        slot_grads = block_dot(gated, loss_grads, ((2,), (1,))).reshape(n * capacity, width)
        hidden_grad = lax.dot_general(slot_grads, w_down[0], contract_last, preferred_element_type=f32)
        sigma = jax.nn.sigmoid(gate_pre)
        gate_grad = (hidden_grad * up_pre * sigma * (1.0 + gate_pre * (1.0 - sigma))).astype(bf16)
        up_grad = (hidden_grad * gate_pre * sigma).astype(bf16)
        row_part = lax.dot_general(gate_grad, w_gate[0], contract_last, preferred_element_type=f32)
        row_part = row_part + lax.dot_general(up_grad, w_up[0], contract_last, preferred_element_type=f32)
        backs = block_dot(select, row_part.astype(bf16).reshape(n, capacity, width), ((1,), (1,)))
    (grad_tokens,) = run(
        functools.partial(return_kernel, n),
        [jax.ShapeDtypeStruct((count, width), bf16)],
        bufs + sems,
        2,
        backs,
    )
    grad_down = lax.dot_general(hidden, slot_grads, contract_first, preferred_element_type=f32)
    grad_gate = lax.dot_general(slot_rows, gate_grad, contract_first, preferred_element_type=f32)
    grad_up = lax.dot_general(slot_rows, up_grad, contract_first, preferred_element_type=f32)
    return grad_tokens, grad_gate[None], grad_up[None], grad_down[None]


def solution(mesh):
    return jax.shard_map(
        shards,
        mesh=mesh,
        in_specs=(
            P("expert", None),
            P("expert", None),
            P("expert", None),
            P("expert"),
            P(),
            P("expert", None),
            P("expert", None, "dp"),
            P("expert", None, "dp"),
            P("expert", "dp", None),
        ),
        out_specs=(
            P("expert", None),
            P("expert", None, "dp"),
            P("expert", None, "dp"),
            P("expert", "dp", None),
        ),
        check_vma=False,
    )
```
